512 devices in a mesh: expert: 32 (over z, core), dp: 16 (over x, y).
Axes of the slice: x: 4, y: 4, z: 16, core: 2. Of those that a mesh axis runs over, the one named last changes fastest.
Arguments:
- tokens: bfloat16 [8192, 7168], P('expert', 'dp'), may hold values from -6 to 6
- cotangent: bfloat16 [8192, 7168], P('expert', 'dp'), may hold values from -6 to 6
- gate_weight: bfloat16 [32, 7168, 1024], P('expert', 'dp'), may hold values from -0.0625 to 0.0625
- up_weight: bfloat16 [32, 7168, 1024], P('expert', 'dp'), may hold values from -0.0625 to 0.0625
- down_weight: bfloat16 [32, 1024, 7168], P('expert', None, 'dp'), may hold values from -0.1875 to 0.1875
- expert_ids: int32 [8192, 8], P('expert'), may hold values from 0 to 255, all different within a row; in each aligned block of 256 rows (0 to 255, 256 to 511, ...) at most 16 rows name the same one
- gate_values: float32 [8192, 8], P('expert'), may hold values from 0.05 to 0.5
Outputs:
- token_grad: bfloat16 [8192, 7168], P('expert', 'dp')
- gate_grad: bfloat16 [32, 7168, 1024], P('expert', 'dp')
- up_grad: bfloat16 [32, 7168, 1024], P('expert', 'dp')
The draws below stay inside these ranges and needn't reach their ends.
Inputs may be any that keep to these rules, and one draw needn't show every extreme that they name: `expert_ids`: each row names 8 different experts. Among the 256 rows of one index of expert no expert is named more than 16 times, and in every draw some expert is named exactly 16 times there; loads are skewed.
All inputs are finite; a program needn't handle non-finite values.
Results may differ from the reference program's by a relative error of at most 0.0058.
Values may be sent and summed in bfloat16 or wider, within the bound.
No kernel may reach another device: no remote copies, remote signals or barrier semaphores. Data moves between devices by JAX's collectives and lax.ppermute only.
A program may use at most 64 MiB of HBM per device.

```python
import math
import jax
import jax.numpy as jnp
import numpy as np
from jax import lax

D = 7168
FF = 1024
EXPERTS_ALL = 256
TOP = 8
TOK_G = 256
CAP = 16
EXP_WIN = 32
TOKENS = 8192
N_EXPERT = 32


def levels(stream_key, shape, cuts, smallest, largest):
    gain = 1.0
    for dim, parts in cuts:
        steps = jax.random.uniform(jax.random.fold_in(jax.random.fold_in(stream_key, 6), dim), (parts,), jnp.float32, smallest / len(cuts), largest / len(cuts))
        gain = gain * jnp.repeat(jnp.exp(steps), shape[dim] // parts).reshape((-1,) + (1,) * (len(shape) - 1 - dim))
    return gain


def assign_block(stream_key, own, number, rows, amount, top, reach, skew):
    sequence = jax.random.permutation(stream_key, amount)
    crowded, common = load_shares(amount, rows * top, reach, skew, True), load_shares(amount, rows * top, reach, skew, False)
    places = jnp.arange(amount)

    def named(sizes, turn):
        used = int((sizes > 0).sum())
        fixed = max(1, used // 4)
        passed = fixed + (places - fixed + turn * (used - fixed)) % max(1, amount - fixed)
        return jnp.zeros((amount,), jnp.int32).at[sequence[jnp.where(places < fixed, places, passed)]].set(jnp.asarray(sizes, jnp.int32))

    sizes = jnp.where(number % 4 == 0, named(crowded, number // 4), named(common, number - number // 4 - 1))
    mixed = jax.random.permutation(jax.random.fold_in(own, 3), amount)
    source_of, sink = mixed[0:amount // 2 * 2:2], mixed[1:amount // 2 * 2:2]
    margin = jnp.minimum(sizes[source_of] - 1, reach - sizes[sink]) // 2
    margin = jnp.where((source_of == sequence[0]) | (sink == sequence[0]) | (sizes[sink] == 0), 0, jnp.maximum(margin, 0))
    passed = jax.random.randint(jax.random.fold_in(own, 4), (amount // 2,), 0, 1 << 20) % (margin + 1)
    sizes = sizes.at[source_of].add(-passed).at[sink].add(passed)
    members = jnp.searchsorted(jnp.cumsum(sizes), jnp.arange(rows * top), side="right").astype(jnp.int32)
    listing = members.reshape(top, rows).T
    listing = listing[jax.random.permutation(jax.random.fold_in(own, 1), rows)]
    turn = jax.random.randint(jax.random.fold_in(own, 2), (rows, 1), 0, top)
    return jnp.take_along_axis(listing, (jnp.arange(top)[None, :] + turn) % top, axis=1)


def load_shares(amount, total, most, skew, full):
    weights = [(1 << 20) // math.isqrt(grade ** skew) + 1 for grade in range(1, amount + 1)]
    largest = most if full else min(most, max(-(-total // amount), total * weights[0] // sum(weights)))
    least = 1 if total - largest >= amount - 1 else 0
    given, surplus = [largest] + [least] * (amount - 1), total - largest - least * (amount - 1)
    while surplus > 0:
        movable = [i for i in range(1, amount) if given[i] < largest] or [i for i in range(1, amount) if given[i] < most]
        mass, budget = sum([weights[i] for i in movable]), surplus
        for i in movable:
            extra = min(most - given[i], max(1, budget * weights[i] // mass), surplus)
            given[i] = given[i] + extra
            surplus = surplus - extra
    return np.array(given)


def gaussian(own_key, shape, width, most, cuts=(), held_as=jnp.bfloat16):
    drawn = jax.random.normal(own_key, shape, jnp.float32) * width
    if len(cuts) > 0:
        drawn = levels(own_key, shape, cuts, -0.22, 0.18) * drawn
    return jnp.clip(drawn, min=-most, max=most).astype(held_as)


def setup_inputs(seed: int = 0) -> dict:
    arg_keys = jax.random.split(jax.random.key(seed), 8)
    tokens = gaussian(arg_keys[0], (TOKENS, D), 1.0, 6.0, ((0, 32), (1, 16)))
    cotangent = gaussian(arg_keys[1], (TOKENS, D), 1.0, 6.0, ((0, 32), (1, 16)))
    gate_weight = gaussian(arg_keys[2], (EXP_WIN, D, FF), D ** -0.5, 0.0625, ((0, 32), (1, 16)))
    up_weight = gaussian(arg_keys[3], (EXP_WIN, D, FF), D ** -0.5, 0.0625, ((0, 32), (1, 16)))
    down_weight = gaussian(arg_keys[4], (EXP_WIN, FF, D), FF ** -0.5, 0.1875, ((0, 32), (2, 16)))
    expert_ids_keys = jax.random.split(jax.random.fold_in(arg_keys[5], 1), TOKENS // TOK_G)
    expert_ids_turns = jax.random.permutation(jax.random.fold_in(arg_keys[5], 3), TOKENS // TOK_G)
    expert_ids = jax.vmap(lambda own, number: assign_block(jax.random.fold_in(arg_keys[5], 2), own, number, TOK_G, EXPERTS_ALL, TOP, CAP, 2))(expert_ids_keys, expert_ids_turns).reshape((TOKENS, TOP))
    gate_values = jnp.clip(0.05 + 0.45 * jax.random.uniform(arg_keys[6], (TOKENS, TOP), jnp.float32) ** levels(arg_keys[6], (TOKENS, TOP), ((0, 32),), -0.2, 0.2), 0.05, 0.5)
    return dict(tokens=tokens, cotangent=cotangent, gate_weight=gate_weight, up_weight=up_weight, down_weight=down_weight, expert_ids=expert_ids, gate_values=gate_values)


def slot_tables(block_ids, block_gates):
    held = N_EXPERT
    flat_ids = block_ids.reshape(-1)
    flat_gates = block_gates.reshape(-1)
    onehot = (flat_ids[:, None] == jnp.arange(held, dtype=jnp.int32)[None, :]).astype(jnp.int32)
    before = jnp.cumsum(onehot, axis=0) - onehot
    rank = jnp.sum(before * onehot, axis=1).astype(jnp.int32)
    inside = flat_ids < held
    dummy = jnp.int32(held * CAP)
    target = jnp.where(inside, flat_ids * CAP + rank, dummy).astype(jnp.int32)
    token_of_pair = (jnp.arange(TOK_G * TOP, dtype=jnp.int32) // TOP).astype(jnp.int32)
    index_table = jnp.zeros((held * CAP + 1,), jnp.int32).at[target].set(token_of_pair)[:-1]
    weight_table = jnp.zeros((held * CAP + 1,), jnp.float32).at[target].set(flat_gates)[:-1]
    valid_table = jnp.zeros((held * CAP + 1,), jnp.float32).at[target].set(jnp.ones_like(flat_gates))[:-1]
    return index_table, weight_table, valid_table


def reference(tokens, cotangent, gate_weight, up_weight, down_weight, expert_ids, gate_values):
    held = N_EXPERT
    index_table, weight_table, valid_table = jax.vmap(slot_tables)(
        expert_ids.reshape(held, TOK_G, TOP), gate_values.reshape(held, TOK_G, TOP))
    offsets = (jnp.arange(held, dtype=jnp.int32) * TOK_G)[:, None]
    index_table = (index_table + offsets).astype(jnp.int32)

    def by_expert(table):
        return jnp.transpose(table.reshape(held, held, CAP), (1, 0, 2)).reshape(held, held * CAP)

    index_table = by_expert(index_table)
    weight_table = by_expert(weight_table)
    valid_table = by_expert(valid_table)

    def one_expert(total, inputs):
        gate_w, up_w, down_w, index, weight, valid = inputs
        rows = tokens[index] * valid.astype(jnp.bfloat16)[:, None]
        weighted = (weight[:, None] * cotangent[index].astype(jnp.float32)).astype(jnp.bfloat16)
        gate_act = jnp.dot(rows, gate_w, preferred_element_type=jnp.float32)
        up_act = jnp.dot(rows, up_w, preferred_element_type=jnp.float32)
        back_act = jnp.dot(weighted, down_w.T, preferred_element_type=jnp.float32)
        sig = jax.nn.sigmoid(gate_act)
        grad_gate = (back_act * up_act * sig * (1.0 + gate_act * (1.0 - sig))).astype(jnp.bfloat16)
        grad_up = (back_act * gate_act * sig).astype(jnp.bfloat16)
        gate_grad = jnp.dot(rows.T, grad_gate, preferred_element_type=jnp.float32).astype(jnp.bfloat16)
        up_grad = jnp.dot(rows.T, grad_up, preferred_element_type=jnp.float32).astype(jnp.bfloat16)
        row_grads = (jnp.dot(grad_gate, gate_w.T, preferred_element_type=jnp.float32)
                     + jnp.dot(grad_up, up_w.T, preferred_element_type=jnp.float32)).astype(jnp.bfloat16)
        total = total.at[index].add(row_grads.astype(jnp.float32) * valid[:, None])
        return total, (gate_grad, up_grad)

    start = jnp.zeros((TOKENS, D), jnp.float32)
    total, grads = lax.scan(one_expert, start,
                            (gate_weight, up_weight, down_weight, index_table, weight_table, valid_table))
    return total.astype(jnp.bfloat16), grads[0], grads[1]
```

```python
import jax
import jax.numpy as jnp
from jax import lax
from jax.experimental import pallas as pl
from jax.experimental.pallas import tpu as pltpu
from jax.sharding import PartitionSpec as P

CAP = 16
MIB = 1 << 20


def dispatch_kernel(ids_ref, gates_ref, tokens_ref, cotangent_ref, send_ref, member_ref, both):
    tok_rows, top_count = ids_ref.shape
    width = tokens_ref.shape[1]
    slots = send_ref.shape[0]
    held = slots // CAP
    ids = ids_ref[...]
    gates = gates_ref[...]
    lane = lax.broadcasted_iota(jnp.int32, (tok_rows, 128), 1)
    onehot = jnp.zeros((tok_rows, 128), jnp.float32)
    gate = jnp.zeros((tok_rows, 128), jnp.float32)
    for k in range(top_count):
        hit = ids[:, k : k + 1] == lane
        onehot = jnp.where(hit, 1.0, onehot)
        gate = jnp.where(hit, gates[:, k : k + 1], gate)
    named = onehot.T[:held]
    gate = gate.T[:held]
    earlier = lax.broadcasted_iota(jnp.int32, (tok_rows, tok_rows), 0) < lax.broadcasted_iota(
        jnp.int32, (tok_rows, tok_rows), 1
    )
    rank = jnp.dot(
        named.astype(jnp.bfloat16),
        jnp.where(earlier, 1.0, 0.0).astype(jnp.bfloat16),
        preferred_element_type=jnp.float32,
    )
    code = jnp.where(named > 0.0, rank, -1.0)

    def by_slot(table):
        return jnp.broadcast_to(table[:, None, :], (held, CAP, tok_rows)).reshape(slots, tok_rows)

    slot = (lax.broadcasted_iota(jnp.int32, (slots, tok_rows), 0) % CAP).astype(jnp.float32)
    placed = by_slot(code) == slot
    slot_gate = jnp.sum(jnp.where(placed, by_slot(gate), 0.0), axis=1, keepdims=True)
    member = jnp.where(placed, 1.0, 0.0).astype(jnp.bfloat16)
    member_ref[...] = member
    both[:, :width] = tokens_ref[...]
    both[:, width:] = cotangent_ref[...]
    picked = jnp.dot(member, both[...], preferred_element_type=jnp.float32)
    column = lax.broadcasted_iota(jnp.int32, picked.shape, 1)
    send_ref[...] = jnp.where(column < width, picked, picked * slot_gate).astype(jnp.bfloat16)


def partial_kernel(scale, recv_ref, gate_ref, up_ref, down_ref, out_ref):
    width = gate_ref.shape[0]
    parts, _, rows, cols = out_ref.shape
    x = recv_ref[:, :width]
    g = recv_ref[:, width:]

    def put(i, value):
        out_ref[:, i] = (value * scale).astype(out_ref.dtype).reshape(parts, rows, cols)

    put(0, jnp.dot(x, gate_ref[...], preferred_element_type=jnp.float32))
    put(1, jnp.dot(x, up_ref[...], preferred_element_type=jnp.float32))
    put(
        2,
        lax.dot_general(
            g, down_ref[...], (((1,), (1,)), ((), ())), preferred_element_type=jnp.float32
        ),
    )


def local_kernel(scale, parts_ref, out_ref):
    parts, _, rows, cols = parts_ref.shape

    def total(i):
        value = parts_ref[0, i].astype(jnp.float32)
        for p in range(1, parts):
            value = value + parts_ref[p, i].astype(jnp.float32)
        return value * scale

    gate_act, up_act, back_act = total(0), total(1), total(2)
    sig = 1.0 / (1.0 + jnp.exp(-gate_act))
    back_sig = back_act * sig
    grad_gate = (back_act * up_act * sig * (1.0 + gate_act * (1.0 - sig))).astype(jnp.bfloat16)
    grad_up = (back_act * gate_act * sig).astype(jnp.bfloat16)
    for p in range(out_ref.shape[0]):
        out_ref[p, 0] = grad_gate
        out_ref[p, 1] = grad_up


def body(tokens, cotangent, gate_weight, up_weight, down_weight, expert_ids, gate_values):
    held = lax.axis_size("expert")
    parts = lax.axis_size("dp")
    tok_rows, width = tokens.shape
    slots = held * CAP
    hidden = gate_weight.shape[2]
    gate_w = gate_weight[0]
    up_w = up_weight[0]
    down_w = down_weight[0]
    send, member = pl.pallas_call(
        dispatch_kernel,
        out_shape=(
            jax.ShapeDtypeStruct((slots, 2 * width), jnp.bfloat16),
            jax.ShapeDtypeStruct((slots, tok_rows), jnp.bfloat16),
        ),
        scratch_shapes=[pltpu.VMEM((tok_rows, 2 * width), jnp.bfloat16)],
        compiler_params=pltpu.CompilerParams(vmem_limit_bytes=32 * MIB),
        name="dispatch",
    )(expert_ids, gate_values, tokens, cotangent)
    recv = lax.all_to_all(
        send.reshape(held, CAP, 2 * width), "expert", split_axis=0, concat_axis=0, tiled=True
    ).reshape(slots, 2 * width)
    rows = slots // parts
    tile = 256
    sums = pl.pallas_call(
        lambda *refs: partial_kernel(1.0, *refs),
        grid=(hidden // tile,),
        in_specs=[
            pl.BlockSpec((slots, 2 * width), lambda i: (0, 0)),
            pl.BlockSpec((width, tile), lambda i: (0, i)),
            pl.BlockSpec((width, tile), lambda i: (0, i)),
            pl.BlockSpec((tile, width), lambda i: (i, 0)),
        ],
        out_specs=pl.BlockSpec((parts, 3, rows, tile), lambda i: (0, 0, 0, i)),
        out_shape=jax.ShapeDtypeStruct((parts, 3, rows, hidden), SENT),
        compiler_params=pltpu.CompilerParams(vmem_limit_bytes=32 * MIB),
        name="partials",
    )(recv, gate_w, up_w, down_w)
    sums = lax.all_to_all(sums, "dp", split_axis=0, concat_axis=0, tiled=True)
    grads = pl.pallas_call(
        lambda *refs: local_kernel(1.0, *refs),
        grid=(hidden // tile,),
        in_specs=[pl.BlockSpec((parts, 3, rows, tile), lambda i: (0, 0, 0, i))],
        out_specs=pl.BlockSpec((parts, 2, rows, tile), lambda i: (0, 0, 0, i)),
        out_shape=jax.ShapeDtypeStruct((parts, 2, rows, hidden), jnp.bfloat16),
        compiler_params=pltpu.CompilerParams(vmem_limit_bytes=32 * MIB),
        name="local_grads",
    )(sums)
    grads = lax.all_to_all(grads, "dp", split_axis=0, concat_axis=0, tiled=True)
    grad_gate = grads[:, 0].reshape(slots, hidden)
    grad_up = grads[:, 1].reshape(slots, hidden)
    row_grads = (
        lax.dot_general(
            grad_gate, gate_w, (((1,), (1,)), ((), ())), preferred_element_type=jnp.float32
        )
        + lax.dot_general(
            grad_up, up_w, (((1,), (1,)), ((), ())), preferred_element_type=jnp.float32
        )
    ).astype(jnp.bfloat16)
    returned = lax.all_to_all(
        row_grads.reshape(held, CAP, width), "expert", split_axis=0, concat_axis=0, tiled=True
    ).reshape(slots, width)
    recv_rows = recv[:, :width]
    gate_grad = lax.dot_general(
        recv_rows, grad_gate, (((0,), (0,)), ((), ())), preferred_element_type=jnp.float32
    ).astype(jnp.bfloat16)
    up_grad = lax.dot_general(
        recv_rows, grad_up, (((0,), (0,)), ((), ())), preferred_element_type=jnp.float32
    ).astype(jnp.bfloat16)
    token_grad = lax.dot_general(
        member, returned, (((0,), (0,)), ((), ())), preferred_element_type=jnp.float32
    ).astype(jnp.bfloat16)
    return (token_grad, gate_grad[None], up_grad[None])


SENT = jnp.bfloat16


def solution(mesh):
    placed = (
        P("expert", "dp"),
        P("expert", "dp"),
        P("expert", "dp", None),
        P("expert", "dp", None),
        P("expert", None, "dp"),
        P("expert", None),
        P("expert", None),
    )
    return jax.shard_map(
        body,
        mesh=mesh,
        in_specs=placed,
        out_specs=(P("expert", "dp"), P("expert", "dp", None), P("expert", "dp", None)),
        check_vma=False,
    )
```

```python
import jax
import jax.numpy as jnp
from jax import lax
from jax.experimental import pallas as pl
from jax.experimental.pallas import tpu as pltpu
from jax.sharding import PartitionSpec as P

CAP = 16
MIB = 1 << 20


def dispatch_kernel(
    ids_hbm, gates_hbm, tokens_hbm, cotangent_hbm, send_ref, member_ref,
    ids_ref, gates_ref, tokens_ref, cotangent_ref, both, sems,
):
    copies = [
        pltpu.make_async_copy(source, target, sems.at[i])
        for i, (source, target) in enumerate(
            (
                (ids_hbm, ids_ref),
                (gates_hbm, gates_ref),
                (tokens_hbm, tokens_ref),
                (cotangent_hbm, cotangent_ref),
            )
        )
    ]
    for copy in copies:
        copy.start()
    tok_rows, top_count = ids_ref.shape
    width = tokens_ref.shape[1]
    slots = send_ref.shape[0]
    held = slots // CAP
    copies[0].wait()
    copies[1].wait()
    ids = ids_ref[...]
    gates = gates_ref[...]
    lane = lax.broadcasted_iota(jnp.int32, (tok_rows, 128), 1)
    onehot = jnp.zeros((tok_rows, 128), jnp.float32)
    gate = jnp.zeros((tok_rows, 128), jnp.float32)
    for k in range(top_count):
        hit = ids[:, k : k + 1] == lane
        onehot = jnp.where(hit, 1.0, onehot)
        gate = jnp.where(hit, gates[:, k : k + 1], gate)
    named = onehot.T[:held]
    gate = gate.T[:held]
    earlier = lax.broadcasted_iota(jnp.int32, (tok_rows, tok_rows), 0) < lax.broadcasted_iota(
        jnp.int32, (tok_rows, tok_rows), 1
    )
    rank = jnp.dot(
        named.astype(jnp.bfloat16),
        jnp.where(earlier, 1.0, 0.0).astype(jnp.bfloat16),
        preferred_element_type=jnp.float32,
    )
    code = jnp.where(named > 0.0, rank, -1.0)

    def by_slot(table):
        return jnp.broadcast_to(table[:, None, :], (held, CAP, tok_rows)).reshape(slots, tok_rows)

    slot = (lax.broadcasted_iota(jnp.int32, (slots, tok_rows), 0) % CAP).astype(jnp.float32)
    placed = by_slot(code) == slot
    slot_gate = jnp.sum(jnp.where(placed, by_slot(gate), 0.0), axis=1, keepdims=True)
    member = jnp.where(placed, 1.0, 0.0).astype(jnp.bfloat16)
    member_ref[...] = member
    copies[2].wait()
    copies[3].wait()
    both[:, :width] = tokens_ref[...]
    both[:, width:] = cotangent_ref[...]
    picked = jnp.dot(member, both[...], preferred_element_type=jnp.float32)
    column = lax.broadcasted_iota(jnp.int32, picked.shape, 1)
    send_ref[...] = jnp.where(column < width, picked, picked * slot_gate).astype(jnp.bfloat16)


def scale_power(value):
    most = jnp.max(jnp.abs(value), axis=1, keepdims=True)
    return jnp.floor(jnp.log2(jnp.maximum(most, 1e-30)))


def put_coded(out_ref, at, values):
    rows, cols = values[0].shape
    lane = lax.broadcasted_iota(jnp.int32, (rows, 128), 1)
    powers = jnp.zeros((rows, 128), jnp.float32)
    for i, value in enumerate(values):
        power = scale_power(value)
        coded = jnp.round(value * jnp.exp2(13.0 - power)).astype(jnp.int32).astype(jnp.int16)
        out_ref[at, i * cols : (i + 1) * cols] = coded
        powers = jnp.where(lane == i, power, powers)
    out_ref[at, 3 * cols :] = powers.astype(jnp.int32).astype(jnp.int16)


def sum_coded(parts_ref, cols):
    totals = [None] * 3
    for p in range(parts_ref.shape[0]):
        powers = parts_ref[p, :, 3 * cols :].astype(jnp.int32).astype(jnp.float32)
        for i in range(3):
            unit = jnp.exp2(powers[:, i : i + 1] - 13.0)
            coded = parts_ref[p, :, i * cols : (i + 1) * cols].astype(jnp.int32)
            value = coded.astype(jnp.float32) * unit
            totals[i] = value if p == 0 else totals[i] + value
    return totals


def partial_kernel(recv_ref, gate_ref, up_ref, down_ref, out_ref):
    width = gate_ref.shape[0]
    x = recv_ref[:, :width]
    g = recv_ref[:, width:]
    values = (
        jnp.dot(x, gate_ref[...], preferred_element_type=jnp.float32),
        jnp.dot(x, up_ref[...], preferred_element_type=jnp.float32),
        lax.dot_general(
            g, down_ref[...], (((1,), (1,)), ((), ())), preferred_element_type=jnp.float32
        ),
    )
    put_coded(out_ref, slice(None), values)


def middle_kernel(cols, parts_ref, out_ref):
    put_coded(out_ref, slice(None), sum_coded(parts_ref, cols))


def local_kernel(cols, parts_ref, out_ref):
    gate_act, up_act, back_act = sum_coded(parts_ref, cols)
    sig = 1.0 / (1.0 + jnp.exp(-gate_act))
    grad_gate = (back_act * up_act * sig * (1.0 + gate_act * (1.0 - sig))).astype(jnp.bfloat16)
    grad_up = (back_act * gate_act * sig).astype(jnp.bfloat16)
    for p in range(out_ref.shape[0]):
        out_ref[p, :, :cols] = grad_gate
        out_ref[p, :, cols:] = grad_up


def row_kernel(grads_ref, gate_ref, up_ref, out_ref):
    hidden = gate_ref.shape[1]
    across = (((1,), (1,)), ((), ()))
    out_ref[...] = (
        lax.dot_general(
            grads_ref[:, :hidden], gate_ref[...], across, preferred_element_type=jnp.float32
        )
        + lax.dot_general(
            grads_ref[:, hidden:], up_ref[...], across, preferred_element_type=jnp.float32
        )
    ).astype(jnp.bfloat16)


def plane_groups(held, side, swap):
    groups = []
    for e in range(held):
        for other in range(side):
            if (e % 2 == 1) == swap:
                group = [(e * side + a) * side + other for a in range(side)]
            else:
                group = [(e * side + other) * side + a for a in range(side)]
            groups.append(group)
    return groups


def exchange(blocks, axes, groups):
    return lax.all_to_all(
        blocks, axes, split_axis=0, concat_axis=0, tiled=True, axis_index_groups=groups
    )


def body(tokens, cotangent, gate_weight, up_weight, down_weight, expert_ids, gate_values):
    held = lax.axis_size("expert")
    parts = lax.axis_size("dp")
    tok_rows, width = tokens.shape
    slots = held * CAP
    hidden = gate_weight.shape[2]
    gate_w = gate_weight[0]
    up_w = up_weight[0]
    down_w = down_weight[0]
    send, member = pl.pallas_call(
        dispatch_kernel,
        out_shape=(
            jax.ShapeDtypeStruct((slots, 2 * width), jnp.bfloat16),
            jax.ShapeDtypeStruct((slots, tok_rows), jnp.bfloat16),
        ),
        in_specs=[pl.BlockSpec(memory_space=pltpu.HBM)] * 4,
        scratch_shapes=[
            pltpu.VMEM(expert_ids.shape, expert_ids.dtype),
            pltpu.VMEM(gate_values.shape, gate_values.dtype),
            pltpu.VMEM(tokens.shape, tokens.dtype),
            pltpu.VMEM(cotangent.shape, cotangent.dtype),
            pltpu.VMEM((tok_rows, 2 * width), jnp.bfloat16),
            pltpu.SemaphoreType.DMA((4,)),
        ],
        compiler_params=pltpu.CompilerParams(vmem_limit_bytes=32 * MIB),
        name="dispatch",
    )(expert_ids, gate_values, tokens, cotangent)
    recv = lax.all_to_all(
        send.reshape(held, CAP, 2 * width), "expert", split_axis=0, concat_axis=0, tiled=True
    ).reshape(slots, 2 * width)
    side = 4
    axes = ("expert", "dp")
    first, second = plane_groups(held, side, False), plane_groups(held, side, True)
    rows = slots // parts
    wide = side * rows
    coded = 3 * hidden + 128
    compiler_params = pltpu.CompilerParams(vmem_limit_bytes=32 * MIB)
    sums = pl.pallas_call(
        partial_kernel,
        grid=(side,),
        in_specs=[
            pl.BlockSpec((wide, 2 * width), lambda i: (i, 0)),
            pl.BlockSpec((width, hidden), lambda i: (0, 0)),
            pl.BlockSpec((width, hidden), lambda i: (0, 0)),
            pl.BlockSpec((hidden, width), lambda i: (0, 0)),
        ],
        out_specs=pl.BlockSpec((wide, coded), lambda i: (i, 0)),
        out_shape=jax.ShapeDtypeStruct((slots, coded), jnp.int16),
        compiler_params=compiler_params,
        name="partials",
    )(recv, gate_w, up_w, down_w)
    sums = exchange(sums.reshape(side, wide, coded), axes, first)
    sums = pl.pallas_call(
        lambda *refs: middle_kernel(hidden, *refs),
        grid=(side,),
        in_specs=[pl.BlockSpec((side, rows, coded), lambda i: (0, i, 0))],
        out_specs=pl.BlockSpec((rows, coded), lambda i: (i, 0)),
        out_shape=jax.ShapeDtypeStruct((wide, coded), jnp.int16),
        compiler_params=compiler_params,
        name="middle_sums",
    )(sums)
    sums = exchange(sums.reshape(side, rows, coded), axes, second)
    grads = pl.pallas_call(
        lambda *refs: local_kernel(hidden, *refs),
        out_shape=jax.ShapeDtypeStruct((side, rows, 2 * hidden), jnp.bfloat16),
        compiler_params=compiler_params,
        name="local_grads",
    )(sums)
    grads = exchange(grads, axes, second).reshape(1, wide, 2 * hidden)
    grads = exchange(jnp.broadcast_to(grads, (side, wide, 2 * hidden)), axes, first)
    grads = grads.reshape(slots, 2 * hidden)
    grad_gate = grads[:, :hidden]
    grad_up = grads[:, hidden:]
    half = slots // 2
    row_grads = pl.pallas_call(
        row_kernel,
        grid=(2,),
        in_specs=[
            pl.BlockSpec((half, 2 * hidden), lambda i: (i, 0)),
            pl.BlockSpec((width, hidden), lambda i: (0, 0)),
            pl.BlockSpec((width, hidden), lambda i: (0, 0)),
        ],
        out_specs=pl.BlockSpec((half, width), lambda i: (i, 0)),
        out_shape=jax.ShapeDtypeStruct((slots, width), jnp.bfloat16),
        compiler_params=compiler_params,
        name="row_grads",
    )(grads, gate_w, up_w)
    returned = lax.all_to_all(
        row_grads.reshape(held, CAP, width), "expert", split_axis=0, concat_axis=0, tiled=True
    ).reshape(slots, width)
    recv_rows = recv[:, :width]
    gate_grad = lax.dot_general(
        recv_rows, grad_gate, (((0,), (0,)), ((), ())), preferred_element_type=jnp.float32
    ).astype(jnp.bfloat16)
    up_grad = lax.dot_general(
        recv_rows, grad_up, (((0,), (0,)), ((), ())), preferred_element_type=jnp.float32
    ).astype(jnp.bfloat16)
    token_grad = lax.dot_general(
        member, returned, (((0,), (0,)), ((), ())), preferred_element_type=jnp.float32
    ).astype(jnp.bfloat16)
    return (token_grad, gate_grad[None], up_grad[None])


def solution(mesh):
    placed = (
        P("expert", "dp"),
        P("expert", "dp"),
        P("expert", "dp", None),
        P("expert", "dp", None),
        P("expert", None, "dp"),
        P("expert", None),
        P("expert", None),
    )
    return jax.shard_map(
        body,
        mesh=mesh,
        in_specs=placed,
        out_specs=(P("expert", "dp"), P("expert", "dp", None), P("expert", "dp", None)),
        check_vma=False,
    )
```

```python
import jax
import jax.numpy as jnp
from jax import lax
from jax.experimental import pallas as pl
from jax.experimental.pallas import tpu as pltpu
from jax.sharding import PartitionSpec as P

CAP = 16
SIDE = 4
TILE = 256
MIB = 1 << 20
AXES = ("expert", "dp")
ACROSS = (((1,), (1,)), ((), ()))
DOWN = (((0,), (0,)), ((), ()))


def dispatch_kernel(ids_ref, gates_ref, tokens_ref, cotangent_ref, send_ref, member_ref, both):
    top_count, tok_rows = ids_ref.shape
    width = tokens_ref.shape[0]
    slots = send_ref.shape[0]
    held = slots // CAP
    ids = ids_ref[...]
    gates = gates_ref[...]
    expert = lax.broadcasted_iota(jnp.int32, (held, tok_rows), 0)
    named = jnp.zeros((held, tok_rows), jnp.float32)
    gate = jnp.zeros((held, tok_rows), jnp.float32)
    for k in range(top_count):
        hit = ids[k : k + 1, :] == expert
        named = jnp.where(hit, 1.0, named)
        gate = jnp.where(hit, gates[k : k + 1, :], gate)
    earlier = lax.broadcasted_iota(jnp.int32, (tok_rows, tok_rows), 0) < lax.broadcasted_iota(
        jnp.int32, (tok_rows, tok_rows), 1
    )
    rank = jnp.dot(
        named.astype(jnp.bfloat16),
        jnp.where(earlier, 1.0, 0.0).astype(jnp.bfloat16),
        preferred_element_type=jnp.float32,
    )
    code = jnp.where(named > 0.0, rank, -1.0)

    def by_slot(table):
        return jnp.broadcast_to(table[:, None, :], (held, CAP, tok_rows)).reshape(slots, tok_rows)

    slot = (lax.broadcasted_iota(jnp.int32, (slots, tok_rows), 0) % CAP).astype(jnp.float32)
    placed = by_slot(code) == slot
    slot_gate = jnp.sum(jnp.where(placed, by_slot(gate), 0.0), axis=1, keepdims=True)
    member = jnp.where(placed, 1.0, 0.0)
    halves = member.reshape(held, 2, CAP // 2, tok_rows)
    for i in (0, 1):
        member_ref[i] = halves[:, i].reshape(slots // 2, tok_rows).astype(jnp.bfloat16)
    member = member.astype(jnp.bfloat16)
    both[:width, :] = tokens_ref[...]
    both[width:, :] = cotangent_ref[...]
    picked = lax.dot_general(member, both[...], ACROSS, preferred_element_type=jnp.float32)
    column = lax.broadcasted_iota(jnp.int32, picked.shape, 1)
    send_ref[...] = jnp.where(column < width, picked, picked * slot_gate).astype(jnp.bfloat16)


def put_coded(out_ref, values):
    rows, cols = values[0].shape
    lane = lax.broadcasted_iota(jnp.int32, (rows, 128), 1)
    powers = jnp.zeros((rows, 128), jnp.float32)
    for i, value in enumerate(values):
        most = jnp.max(jnp.abs(value), axis=1, keepdims=True)
        power = jnp.floor(jnp.log2(jnp.maximum(most, 1e-30)))
        coded = jnp.round(value * jnp.exp2(13.0 - power)).astype(jnp.int32).astype(jnp.int16)
        out_ref[:, i * cols : (i + 1) * cols] = coded
        powers = jnp.where(lane == i, power, powers)
    out_ref[:, 3 * cols :] = powers.astype(jnp.int32).astype(jnp.int16)


def sum_coded(parts_ref, start, cols):
    totals = [None] * 3
    for p in range(parts_ref.shape[0]):
        stop = start + 3 * cols
        powers = parts_ref[p, :, stop : stop + 128].astype(jnp.int32).astype(jnp.float32)
        for i in range(3):
            at = start + i * cols
            unit = jnp.exp2(powers[:, i : i + 1] - 13.0)
            coded = parts_ref[p, :, at : at + cols].astype(jnp.int32)
            value = coded.astype(jnp.float32) * unit
            totals[i] = value if p == 0 else totals[i] + value
    return totals


def partial_kernel(rows_ref, weights_ref, out_ref, x_ref, g_ref):
    parts = rows_ref.shape[0]
    width = rows_ref.shape[2] // 2

    @pl.when(pl.program_id(0) == 0)
    def _():
        for p in range(parts):
            x_ref[:, p * width : (p + 1) * width] = rows_ref[p, :, :width]
            g_ref[:, p * width : (p + 1) * width] = rows_ref[p, :, width:]

    def product(rows, which):
        weight = weights_ref[:, which].reshape(parts * width, TILE)
        return jnp.dot(rows, weight, preferred_element_type=jnp.float32)

    x = x_ref[...]
    put_coded(out_ref, (product(x, 0), product(x, 1), product(g_ref[...], 2)))


def local_kernel(hidden, parts_ref, out_ref):
    for tile in range(hidden // TILE):
        gate_act, up_act, back_act = sum_coded(parts_ref, tile * (3 * TILE + 128), TILE)
        sig = 1.0 / (1.0 + jnp.exp(-gate_act))
        grad_gate = (back_act * up_act * sig * (1.0 + gate_act * (1.0 - sig))).astype(jnp.bfloat16)
        grad_up = (back_act * gate_act * sig).astype(jnp.bfloat16)
        at = tile * TILE
        for p in range(out_ref.shape[0]):
            out_ref[p, :, at : at + TILE] = grad_gate
            out_ref[p, :, hidden + at : hidden + at + TILE] = grad_up


def row_kernel(grads_ref, weights_ref, out_ref):
    width, hidden = weights_ref.shape[2:]

    def product(which):
        grad = grads_ref[:, which * hidden : (which + 1) * hidden]
        return lax.dot_general(
            grad, weights_ref[0, which], ACROSS, preferred_element_type=jnp.float32
        )

    both = (product(0) + product(1)).reshape(-1, 2, CAP // 2, width)
    pair = [both[:, i].reshape(-1, width) for i in (0, 1)]
    out_ref[0] = jnp.concatenate(pair, axis=1).astype(jnp.bfloat16)


def combine_kernel(returned_ref, member_ref, out_ref):
    width = out_ref.shape[0]
    out_ref[...] = (
        lax.dot_general(
            returned_ref[:, :width], member_ref[0], DOWN, preferred_element_type=jnp.float32
        )
        + lax.dot_general(
            returned_ref[:, width:], member_ref[1], DOWN, preferred_element_type=jnp.float32
        )
    ).astype(jnp.bfloat16)


def plane_groups(held, swap):
    groups = []
    for e in range(held):
        for other in range(SIDE):
            if (e % 2 == 1) == swap:
                group = [(e * SIDE + a) * SIDE + other for a in range(SIDE)]
            else:
                group = [(e * SIDE + other) * SIDE + a for a in range(SIDE)]
            groups.append(group)
    return groups


def exchange(blocks, groups):
    return lax.all_to_all(
        blocks, AXES, split_axis=0, concat_axis=0, tiled=True, axis_index_groups=groups
    )


def gather(block, groups):
    return lax.all_gather(block, AXES, axis=0, tiled=True, axis_index_groups=groups)


def body(tokens, cotangent, gate_weight, up_weight, down_weight, expert_ids, gate_values):
    held = lax.axis_size("expert")
    tok_rows, width = tokens.shape
    slots = held * CAP
    hidden = gate_weight.shape[2]
    first, second = plane_groups(held, False), plane_groups(held, True)
    wide = slots // SIDE
    rows = wide // SIDE
    spread = SIDE * width
    coded = hidden // TILE * (3 * TILE + 128)
    params = pltpu.CompilerParams(vmem_limit_bytes=32 * MIB)
    streaming = pltpu.CompilerParams(vmem_limit_bytes=56 * MIB)

    weights = jnp.stack([gate_weight[0], up_weight[0], down_weight[0].T])[None]
    weights = gather(weights, first)

    send, member = pl.pallas_call(
        dispatch_kernel,
        out_shape=(
            jax.ShapeDtypeStruct((slots, 2 * width), jnp.bfloat16),
            jax.ShapeDtypeStruct((2, slots // 2, tok_rows), jnp.bfloat16),
        ),
        scratch_shapes=[pltpu.VMEM((2 * width, tok_rows), jnp.bfloat16)],
        compiler_params=params,
        name="dispatch",
    )(expert_ids.T, gate_values.T, tokens.T, cotangent.T)
    recv = lax.all_to_all(
        send.reshape(held, CAP, 2 * width), "expert", split_axis=0, concat_axis=0, tiled=True
    ).reshape(slots, 2 * width)

    mine = exchange(recv.reshape(SIDE, wide, 2 * width), first)
    sums = pl.pallas_call(
        partial_kernel,
        grid=(hidden // TILE,),
        in_specs=[
            pl.BlockSpec((SIDE, wide, 2 * width), lambda i: (0, 0, 0)),
            pl.BlockSpec((SIDE, 3, width, TILE), lambda i: (0, 0, 0, i)),
        ],
        out_specs=pl.BlockSpec((wide, 3 * TILE + 128), lambda i: (0, i)),
        out_shape=jax.ShapeDtypeStruct((wide, coded), jnp.int16),
        scratch_shapes=[
            pltpu.VMEM((wide, spread), jnp.bfloat16),
            pltpu.VMEM((wide, spread), jnp.bfloat16),
        ],
        compiler_params=streaming,
        name="partials",
    )(mine, weights)
    sums = exchange(sums.reshape(SIDE, rows, coded), second)
    grads = pl.pallas_call(
        lambda *refs: local_kernel(hidden, *refs),
        out_shape=jax.ShapeDtypeStruct((SIDE, rows, 2 * hidden), jnp.bfloat16),
        compiler_params=params,
        name="local_grads",
    )(sums)
    grads = exchange(grads, second).reshape(wide, 2 * hidden)
    row_grads = pl.pallas_call(
        row_kernel,
        grid=(SIDE,),
        in_specs=[
            pl.BlockSpec((wide, 2 * hidden), lambda i: (0, 0)),
            pl.BlockSpec((1, 2, width, hidden), lambda i: (i, 0, 0, 0)),
        ],
        out_specs=pl.BlockSpec((1, wide // 2, 2 * width), lambda i: (i, 0, 0)),
        out_shape=jax.ShapeDtypeStruct((SIDE, wide // 2, 2 * width), jnp.bfloat16),
        compiler_params=streaming,
        name="row_grads",
    )(grads, weights)
    row_grads = exchange(row_grads, first)
    returned = lax.all_to_all(
        row_grads.reshape(held, CAP // 2, 2 * width),
        "expert",
        split_axis=0,
        concat_axis=0,
        tiled=True,
    ).reshape(slots // 2, 2 * width)

    grads_all = gather(grads, first)
    recv_rows = recv[:, :width]
    gate_grad = lax.dot_general(
        recv_rows, grads_all[:, :hidden], DOWN, preferred_element_type=jnp.float32
    ).astype(jnp.bfloat16)
    up_grad = lax.dot_general(
        recv_rows, grads_all[:, hidden:], DOWN, preferred_element_type=jnp.float32
    ).astype(jnp.bfloat16)
    returned, gate_grad, up_grad = lax.optimization_barrier((returned, gate_grad, up_grad))
    token_grad = pl.pallas_call(
        combine_kernel,
        out_shape=jax.ShapeDtypeStruct((width, tok_rows), jnp.bfloat16),
        compiler_params=params,
        name="combine",
    )(returned, member).T
    return (token_grad, gate_grad[None], up_grad[None])


def solution(mesh):
    placed = (
        P("expert", "dp"),
        P("expert", "dp"),
        P("expert", "dp", None),
        P("expert", "dp", None),
        P("expert", None, "dp"),
        P("expert", None),
        P("expert", None),
    )
    return jax.shard_map(
        body,
        mesh=mesh,
        in_specs=placed,
        out_specs=(P("expert", "dp"), P("expert", "dp", None), P("expert", "dp", None)),
        check_vma=False,
    )
```

```python
import jax
import jax.numpy as jnp
from jax import lax
from jax.experimental import pallas as pl
from jax.experimental.pallas import tpu as pltpu
from jax.sharding import PartitionSpec as P

CAP = 16
SIDE = 4
TILE = 256
MIB = 1 << 20
AXES = ("expert", "dp")
ACROSS = (((1,), (1,)), ((), ()))
DOWN = (((0,), (0,)), ((), ()))
SHIFTS = (0, 3, 1, 2)


def block_at(ref, at):
    block = ref[0]
    for p in range(1, SIDE):
        block = jnp.where(at == p, ref[p], block)
    return block


def pack_kernel(gate_ref, up_ref, down_ref, low_ref, high_ref):
    width = gate_ref.shape[0]
    half = width // 2
    low_ref[:width] = gate_ref[...]
    low_ref[width:] = down_ref[:half]
    high_ref[:width] = up_ref[...]
    high_ref[width:] = down_ref[half:]


def dispatch_kernel(ids_ref, gates_ref, tokens_ref, cotangent_ref, send_ref, member_ref, both):
    top_count, tok_rows = ids_ref.shape
    width = tokens_ref.shape[0]
    slots = send_ref.shape[0]
    held = slots // CAP
    ids = ids_ref[...]
    gates = gates_ref[...]
    expert = lax.broadcasted_iota(jnp.int32, (held, tok_rows), 0)
    named = jnp.zeros((held, tok_rows), jnp.float32)
    gate = jnp.zeros((held, tok_rows), jnp.float32)
    for k in range(top_count):
        hit = ids[k : k + 1, :] == expert
        named = jnp.where(hit, 1.0, named)
        gate = jnp.where(hit, gates[k : k + 1, :], gate)
    earlier = lax.broadcasted_iota(jnp.int32, (tok_rows, tok_rows), 0) < lax.broadcasted_iota(
        jnp.int32, (tok_rows, tok_rows), 1
    )
    rank = jnp.dot(
        named.astype(jnp.bfloat16),
        jnp.where(earlier, 1.0, 0.0).astype(jnp.bfloat16),
        preferred_element_type=jnp.float32,
    )
    code = jnp.where(named > 0.0, rank, -1.0)

    def by_slot(table):
        return jnp.broadcast_to(table[:, None, :], (held, CAP, tok_rows)).reshape(slots, tok_rows)

    slot = (lax.broadcasted_iota(jnp.int32, (slots, tok_rows), 0) % CAP).astype(jnp.float32)
    placed = by_slot(code) == slot
    slot_gate = jnp.sum(jnp.where(placed, by_slot(gate), 0.0), axis=1, keepdims=True)
    member = jnp.where(placed, 1.0, 0.0)
    halves = member.reshape(held, 2, CAP // 2, tok_rows)
    for i in (0, 1):
        member_ref[i] = halves[:, i].reshape(slots // 2, tok_rows).astype(jnp.bfloat16)
    member = member.astype(jnp.bfloat16)
    both[:width, :] = tokens_ref[...]
    both[width:, :] = cotangent_ref[...]
    picked = lax.dot_general(member, both[...], ACROSS, preferred_element_type=jnp.float32)
    column = lax.broadcasted_iota(jnp.int32, picked.shape, 1)
    send_ref[...] = jnp.where(column < width, picked, picked * slot_gate).astype(jnp.bfloat16)


def put_coded(out_ref, values):
    rows, cols = values[0].shape
    lane = lax.broadcasted_iota(jnp.int32, (rows, 128), 1)
    powers = jnp.zeros((rows, 128), jnp.float32)
    for i, value in enumerate(values):
        most = jnp.max(jnp.abs(value), axis=1, keepdims=True)
        power = jnp.floor(jnp.log2(jnp.maximum(most, 1e-30)))
        coded = jnp.round(value * jnp.exp2(13.0 - power)).astype(jnp.int32).astype(jnp.int16)
        out_ref[:, i * cols : (i + 1) * cols] = coded
        powers = jnp.where(lane == i, power, powers)
    out_ref[:, 3 * cols :] = powers.astype(jnp.int32).astype(jnp.int16)


def sum_coded(parts_ref, cols):
    totals = [None] * 3
    for p in range(parts_ref.shape[0]):
        powers = parts_ref[p, :, 3 * cols :].astype(jnp.int32).astype(jnp.float32)
        for i in range(3):
            unit = jnp.exp2(powers[:, i : i + 1] - 13.0)
            coded = parts_ref[p, :, i * cols : (i + 1) * cols].astype(jnp.int32)
            value = coded.astype(jnp.float32) * unit
            totals[i] = value if p == 0 else totals[i] + value
    return totals


def partial_kernel(place_ref, rows_ref, *refs):
    lows, highs = refs[:SIDE], refs[SIDE : 2 * SIDE]
    out_ref = refs[2 * SIDE]
    width = rows_ref.shape[2] // 2
    half = width // 2
    totals = [None] * 3

    def add(which, rows, weight):
        value = jnp.dot(rows, weight, preferred_element_type=jnp.float32)
        totals[which] = value if totals[which] is None else totals[which] + value

    for shift, low, high in zip(SHIFTS, lows, highs):
        both = block_at(rows_ref, lax.rem(place_ref[0] + shift, SIDE))
        x = both[:, :width]
        add(0, x, low[:width])
        add(1, x, high[:width])
        add(2, both[:, width : width + half], low[width:])
        add(2, both[:, width + half :], high[width:])
    put_coded(out_ref, totals)


def local_kernel(hidden, parts_ref, out_ref):
    gate_act, up_act, back_act = sum_coded(parts_ref, hidden)
    sig = 1.0 / (1.0 + jnp.exp(-gate_act))
    grad_gate = (back_act * up_act * sig * (1.0 + gate_act * (1.0 - sig))).astype(jnp.bfloat16)
    grad_up = (back_act * gate_act * sig).astype(jnp.bfloat16)
    for p in range(out_ref.shape[0]):
        out_ref[p, :, :hidden] = grad_gate
        out_ref[p, :, hidden:] = grad_up


def row_kernel(place_ref, grads_ref, *refs):
    lows, highs = refs[:SIDE], refs[SIDE : 2 * SIDE]
    out_ref = refs[2 * SIDE]
    wide, hidden = grads_ref.shape[0], grads_ref.shape[1] // 2
    width = out_ref.shape[2] // 2
    for shift, low, high in zip(SHIFTS, lows, highs):
        total = lax.dot_general(
            grads_ref[:, :hidden], low[:width], ACROSS, preferred_element_type=jnp.float32
        ) + lax.dot_general(
            grads_ref[:, hidden:], high[:width], ACROSS, preferred_element_type=jnp.float32
        )
        both = total.reshape(-1, 2, CAP // 2, width)
        pair = [both[:, j].reshape(wide // 2, width) for j in (0, 1)]
        value = jnp.concatenate(pair, axis=1).astype(jnp.bfloat16)
        at = lax.rem(place_ref[0] + shift, SIDE)
        for p in range(SIDE):

            @pl.when(at == p)
            def _():
                out_ref[p] = value


def weight_kernel(place_ref, rows_ref, *refs):
    grads, out_ref = refs[:SIDE], refs[SIDE]
    width = out_ref.shape[1]
    value = None
    for shift, grad in zip(SHIFTS, grads):
        rows = block_at(rows_ref, lax.rem(place_ref[0] + shift, SIDE))[:, :width]
        term = lax.dot_general(rows, grad[...], DOWN, preferred_element_type=jnp.float32)
        value = term if value is None else value + term
    out_ref[0] = value.astype(jnp.bfloat16)


def combine_kernel(returned_ref, member_ref, out_ref):
    width = out_ref.shape[0]
    out_ref[...] = (
        lax.dot_general(
            returned_ref[:, :width], member_ref[0], DOWN, preferred_element_type=jnp.float32
        )
        + lax.dot_general(
            returned_ref[:, width:], member_ref[1], DOWN, preferred_element_type=jnp.float32
        )
    ).astype(jnp.bfloat16)


def plane_groups(held, swap):
    groups = []
    for e in range(held):
        for other in range(SIDE):
            if (e % 2 == 1) == swap:
                group = [(e * SIDE + a) * SIDE + other for a in range(SIDE)]
            else:
                group = [(e * SIDE + other) * SIDE + a for a in range(SIDE)]
            groups.append(group)
    return groups


def plane_ring(held, step):
    pairs = []
    for group in plane_groups(held, False):
        pairs += [(group[i], group[(i + step) % SIDE]) for i in range(SIDE)]
    return pairs


def exchange(blocks, groups):
    return lax.all_to_all(
        blocks, AXES, split_axis=0, concat_axis=0, tiled=True, axis_index_groups=groups
    )


def body(tokens, cotangent, gate_weight, up_weight, down_weight, expert_ids, gate_values):
    held = lax.axis_size("expert")
    tok_rows, width = tokens.shape
    slots = held * CAP
    hidden = gate_weight.shape[2]
    first, second = plane_groups(held, False), plane_groups(held, True)
    wide = slots // SIDE
    rows = wide // SIDE
    coded = 3 * hidden + 128
    params = pltpu.CompilerParams(vmem_limit_bytes=24 * MIB)
    alone = pltpu.CompilerParams(vmem_limit_bytes=48 * MIB)

    onward, back = plane_ring(held, 1), plane_ring(held, -1)
    dp = lax.axis_index("dp")
    place = jnp.where(lax.axis_index("expert") % 2 == 0, dp // SIDE, dp % SIDE)
    place = place.astype(jnp.int32).reshape(1)

    send, member = pl.pallas_call(
        dispatch_kernel,
        out_shape=(
            jax.ShapeDtypeStruct((slots, 2 * width), jnp.bfloat16),
            jax.ShapeDtypeStruct((2, slots // 2, tok_rows), jnp.bfloat16),
        ),
        scratch_shapes=[pltpu.VMEM((2 * width, tok_rows), jnp.bfloat16)],
        compiler_params=alone,
        name="dispatch",
    )(expert_ids.T, gate_values.T, tokens.T, cotangent.T)
    send, gate_w, up_w, down_w = lax.optimization_barrier(
        (send, gate_weight[0], up_weight[0], down_weight[0].T)
    )
    half = jax.ShapeDtypeStruct((width + width // 2, hidden), jnp.bfloat16)
    low, high = pl.pallas_call(
        pack_kernel,
        out_shape=(half, half),
        compiler_params=params,
        name="pack",
    )(gate_w, up_w, down_w)
    low_1 = lax.ppermute(low, AXES, onward)
    high_3 = lax.ppermute(high, AXES, back)
    high_1 = lax.ppermute(high, AXES, onward)
    low_3 = lax.ppermute(low, AXES, back)
    low_2 = lax.ppermute(low_1, AXES, onward)
    high_2 = lax.ppermute(high_3, AXES, back)
    lows, highs = (low, low_1, low_3, low_2), (high, high_1, high_3, high_2)
    recv = lax.all_to_all(
        send.reshape(held, CAP, 2 * width), "expert", split_axis=0, concat_axis=0, tiled=True
    ).reshape(slots, 2 * width)

    mine = exchange(recv.reshape(SIDE, wide, 2 * width), first)
    vmem = pl.BlockSpec(memory_space=pltpu.VMEM)
    smem = pl.BlockSpec(memory_space=pltpu.SMEM)
    sums = pl.pallas_call(
        partial_kernel,
        in_specs=[smem] + [vmem] * (1 + 2 * SIDE),
        out_specs=vmem,
        out_shape=jax.ShapeDtypeStruct((wide, coded), jnp.int16),
        compiler_params=params,
        name="partials",
    )(place, mine, *lows, *highs)
    sums = exchange(sums.reshape(SIDE, rows, coded), second)
    grads = pl.pallas_call(
        lambda *refs: local_kernel(hidden, *refs),
        out_shape=jax.ShapeDtypeStruct((SIDE, rows, 2 * hidden), jnp.bfloat16),
        compiler_params=params,
        name="local_grads",
    )(sums)
    grads = exchange(grads, second).reshape(wide, 2 * hidden)
    row_grads = pl.pallas_call(
        row_kernel,
        in_specs=[smem] + [vmem] * (1 + 2 * SIDE),
        out_specs=vmem,
        out_shape=jax.ShapeDtypeStruct((SIDE, wide // 2, 2 * width), jnp.bfloat16),
        compiler_params=params,
        name="row_grads",
    )(place, grads, *lows, *highs)
    row_grads = exchange(row_grads, first)
    returned = lax.all_to_all(
        row_grads.reshape(held, CAP // 2, 2 * width),
        "expert",
        split_axis=0,
        concat_axis=0,
        tiled=True,
    ).reshape(slots // 2, 2 * width)

    blocks = [grads] + [lax.ppermute(grads, AXES, plane_ring(held, k)) for k in (1, 3, 2)]
    column = 2 * TILE
    per = hidden // column

    def weight_grad(first_column):
        return pl.pallas_call(
            weight_kernel,
            grid=(per,),
            in_specs=[
                pl.BlockSpec(memory_space=pltpu.SMEM),
                pl.BlockSpec((SIDE, wide, 2 * width), lambda i: (0, 0, 0)),
            ]
            + [pl.BlockSpec((wide, column), lambda i: (0, i + first_column))] * SIDE,
            out_specs=pl.BlockSpec((1, width, column), lambda i: (0, 0, i)),
            out_shape=jax.ShapeDtypeStruct((1, width, hidden), jnp.bfloat16),
            compiler_params=params,
            name="weight_grad",
        )(place, recv.reshape(SIDE, wide, 2 * width), *blocks)

    gate_grad, up_grad = weight_grad(0), weight_grad(per)
    returned, gate_grad, up_grad = lax.optimization_barrier((returned, gate_grad, up_grad))
    token_grad = pl.pallas_call(
        combine_kernel,
        out_shape=jax.ShapeDtypeStruct((width, tok_rows), jnp.bfloat16),
        compiler_params=params,
        name="combine",
    )(returned, member).T
    return (token_grad, gate_grad, up_grad)


def solution(mesh):
    placed = (
        P("expert", "dp"),
        P("expert", "dp"),
        P("expert", "dp", None),
        P("expert", "dp", None),
        P("expert", None, "dp"),
        P("expert", None),
        P("expert", None),
    )
    return jax.shard_map(
        body,
        mesh=mesh,
        in_specs=placed,
        out_specs=(P("expert", "dp"), P("expert", "dp", None), P("expert", "dp", None)),
        check_vma=False,
    )
```

```python
import jax
import jax.numpy as jnp
from jax import lax
from jax.experimental import pallas as pl
from jax.experimental.pallas import tpu as pltpu
from jax.sharding import PartitionSpec as P

CAP = 16
SIDE = 4
TILE = 256
MIB = 1 << 20
AXES = ("expert", "dp")
ACROSS = (((1,), (1,)), ((), ()))
DOWN = (((0,), (0,)), ((), ()))
SHIFTS = (0, 3, 1, 2)


def block_at(ref, at):
    block = ref[0]
    for p in range(1, SIDE):
        block = jnp.where(at == p, ref[p], block)
    return block


def pack_kernel(gate_ref, up_ref, down_ref, low_ref, high_ref):
    width = gate_ref.shape[0]
    half = width // 2
    low_ref[:width] = gate_ref[...]
    low_ref[width:] = down_ref[:half]
    high_ref[:width] = up_ref[...]
    high_ref[width:] = down_ref[half:]


def dispatch_kernel(ids_ref, gates_ref, tokens_ref, cotangent_ref, send_ref, member_ref, both):
    top_count, tok_rows = ids_ref.shape
    width = tokens_ref.shape[0]
    slots = send_ref.shape[0]
    held = slots // CAP
    ids = ids_ref[...]
    gates = gates_ref[...]
    expert = lax.broadcasted_iota(jnp.int32, (held, tok_rows), 0)
    named = jnp.zeros((held, tok_rows), jnp.float32)
    gate = jnp.zeros((held, tok_rows), jnp.float32)
    for k in range(top_count):
        hit = ids[k : k + 1, :] == expert
        named = jnp.where(hit, 1.0, named)
        gate = jnp.where(hit, gates[k : k + 1, :], gate)
    earlier = lax.broadcasted_iota(jnp.int32, (tok_rows, tok_rows), 0) < lax.broadcasted_iota(
        jnp.int32, (tok_rows, tok_rows), 1
    )
    rank = jnp.dot(
        named.astype(jnp.bfloat16),
        jnp.where(earlier, 1.0, 0.0).astype(jnp.bfloat16),
        preferred_element_type=jnp.float32,
    )
    code = jnp.where(named > 0.0, rank, -1.0)

    def by_slot(table):
        return jnp.broadcast_to(table[:, None, :], (held, CAP, tok_rows)).reshape(slots, tok_rows)

    slot = (lax.broadcasted_iota(jnp.int32, (slots, tok_rows), 0) % CAP).astype(jnp.float32)
    placed = by_slot(code) == slot
    slot_gate = jnp.sum(jnp.where(placed, by_slot(gate), 0.0), axis=1, keepdims=True)
    member = jnp.where(placed, 1.0, 0.0)
    halves = member.reshape(held, 2, CAP // 2, tok_rows)
    for i in (0, 1):
        member_ref[i] = halves[:, i].reshape(slots // 2, tok_rows).astype(jnp.bfloat16)
    member = member.astype(jnp.bfloat16)
    both[:width, :] = tokens_ref[...]
    both[width:, :] = cotangent_ref[...]
    picked = lax.dot_general(member, both[...], ACROSS, preferred_element_type=jnp.float32)
    column = lax.broadcasted_iota(jnp.int32, picked.shape, 1)
    send_ref[...] = jnp.where(column < width, picked, picked * slot_gate).astype(jnp.bfloat16)


def put_coded(out_ref, values):
    rows, cols = values[0].shape
    lane = lax.broadcasted_iota(jnp.int32, (rows, 128), 1)
    powers = jnp.zeros((rows, 128), jnp.float32)
    for i, value in enumerate(values):
        most = jnp.max(jnp.abs(value), axis=1, keepdims=True)
        power = jnp.floor(jnp.log2(jnp.maximum(most, 1e-30)))
        coded = jnp.round(value * jnp.exp2(13.0 - power)).astype(jnp.int32).astype(jnp.int16)
        out_ref[:, i * cols : (i + 1) * cols] = coded
        powers = jnp.where(lane == i, power, powers)
    out_ref[:, 3 * cols :] = powers.astype(jnp.int32).astype(jnp.int16)


def sum_coded(parts_ref, cols):
    totals = [None] * 3
    for p in range(parts_ref.shape[0]):
        powers = parts_ref[p, :, 3 * cols :].astype(jnp.int32).astype(jnp.float32)
        for i in range(3):
            unit = jnp.exp2(powers[:, i : i + 1] - 13.0)
            coded = parts_ref[p, :, i * cols : (i + 1) * cols].astype(jnp.int32)
            value = coded.astype(jnp.float32) * unit
            totals[i] = value if p == 0 else totals[i] + value
    return totals


def fetch(arrays, buffers, sems):
    copies = []
    for i, (array, buffer) in enumerate(zip(arrays, buffers)):
        source = array.at[: buffer.shape[0]]
        copies.append(pltpu.make_async_copy(source, buffer, sems.at[i]))
        copies[-1].start()

    def ready(i):
        copies[i].wait()
        return buffers[i]

    return ready


def partial_kernel(place_ref, rows_ref, own_low, own_high, *refs):
    others = 2 * (SIDE - 1)
    out_ref = refs[others]
    ready = fetch(refs[:others], refs[others + 1 : -1], refs[-1])
    width = rows_ref.shape[2] // 2
    half = width // 2
    totals = [None] * 3

    def add(which, rows, weight):
        value = jnp.dot(rows, weight, preferred_element_type=jnp.float32)
        totals[which] = value if totals[which] is None else totals[which] + value

    for i, shift in enumerate(SHIFTS):
        both = block_at(rows_ref, lax.rem(place_ref[0] + shift, SIDE))
        x = both[:, :width]
        low = own_low if i == 0 else ready(2 * i - 2)
        add(0, x, low[:width])
        add(2, both[:, width : width + half], low[width:])
        high = own_high if i == 0 else ready(2 * i - 1)
        add(1, x, high[:width])
        add(2, both[:, width + half :], high[width:])
    put_coded(out_ref, totals)


def local_kernel(hidden, parts_ref, out_ref):
    gate_act, up_act, back_act = sum_coded(parts_ref, hidden)
    sig = 1.0 / (1.0 + jnp.exp(-gate_act))
    grad_gate = (back_act * up_act * sig * (1.0 + gate_act * (1.0 - sig))).astype(jnp.bfloat16)
    grad_up = (back_act * gate_act * sig).astype(jnp.bfloat16)
    for p in range(out_ref.shape[0]):
        out_ref[p, :, :hidden] = grad_gate
        out_ref[p, :, hidden:] = grad_up


def row_kernel(place_ref, grads_ref, own_low, own_high, *refs):
    others = 2 * (SIDE - 1)
    out_ref = refs[others]
    ready = fetch(refs[:others], refs[others + 1 : -1], refs[-1])
    wide, hidden = grads_ref.shape[0], grads_ref.shape[1] // 2
    width = out_ref.shape[2] // 2
    values = []
    for i in range(SIDE):
        low = own_low if i == 0 else ready(2 * i - 2)
        total = lax.dot_general(
            grads_ref[:, :hidden], low[:width], ACROSS, preferred_element_type=jnp.float32
        )
        high = own_high if i == 0 else ready(2 * i - 1)
        total = total + lax.dot_general(
            grads_ref[:, hidden:], high[:width], ACROSS, preferred_element_type=jnp.float32
        )
        both = total.reshape(-1, 2, CAP // 2, width)
        pair = [both[:, j].reshape(wide // 2, width) for j in (0, 1)]
        values.append(jnp.concatenate(pair, axis=1).astype(jnp.bfloat16))
    for p in range(SIDE):
        block = values[0]
        for shift, value in zip(SHIFTS[1:], values[1:]):
            block = jnp.where(lax.rem(place_ref[0] + shift, SIDE) == p, value, block)
        out_ref[p] = block


def weight_kernel(place_ref, rows_ref, *refs):
    grads, out_ref = refs[:SIDE], refs[SIDE]
    width = out_ref.shape[1]
    value = None
    for shift, grad in zip(SHIFTS, grads):
        rows = block_at(rows_ref, lax.rem(place_ref[0] + shift, SIDE))[:, :width]
        term = lax.dot_general(rows, grad[...], DOWN, preferred_element_type=jnp.float32)
        value = term if value is None else value + term
    out_ref[0] = value.astype(jnp.bfloat16)


def combine_kernel(returned_ref, member_ref, out_ref):
    width = out_ref.shape[0]
    out_ref[...] = (
        lax.dot_general(
            returned_ref[:, :width], member_ref[0], DOWN, preferred_element_type=jnp.float32
        )
        + lax.dot_general(
            returned_ref[:, width:], member_ref[1], DOWN, preferred_element_type=jnp.float32
        )
    ).astype(jnp.bfloat16)


def plane_groups(held, swap):
    groups = []
    for e in range(held):
        for other in range(SIDE):
            if (e % 2 == 1) == swap:
                group = [(e * SIDE + a) * SIDE + other for a in range(SIDE)]
            else:
                group = [(e * SIDE + other) * SIDE + a for a in range(SIDE)]
            groups.append(group)
    return groups


def plane_ring(held, step):
    pairs = []
    for group in plane_groups(held, False):
        pairs += [(group[i], group[(i + step) % SIDE]) for i in range(SIDE)]
    return pairs


def exchange(blocks, groups):
    return lax.all_to_all(
        blocks, AXES, split_axis=0, concat_axis=0, tiled=True, axis_index_groups=groups
    )


def body(tokens, cotangent, gate_weight, up_weight, down_weight, expert_ids, gate_values):
    held = lax.axis_size("expert")
    tok_rows, width = tokens.shape
    slots = held * CAP
    hidden = gate_weight.shape[2]
    first, second = plane_groups(held, False), plane_groups(held, True)
    wide = slots // SIDE
    rows = wide // SIDE
    coded = 3 * hidden + 128
    params = pltpu.CompilerParams(vmem_limit_bytes=24 * MIB)
    alone = pltpu.CompilerParams(vmem_limit_bytes=56 * MIB)

    onward, back = plane_ring(held, 1), plane_ring(held, -1)
    dp = lax.axis_index("dp")
    place = jnp.where(lax.axis_index("expert") % 2 == 0, dp // SIDE, dp % SIDE)
    place = place.astype(jnp.int32).reshape(1)

    send, member = pl.pallas_call(
        dispatch_kernel,
        out_shape=(
            jax.ShapeDtypeStruct((slots, 2 * width), jnp.bfloat16),
            jax.ShapeDtypeStruct((2, slots // 2, tok_rows), jnp.bfloat16),
        ),
        scratch_shapes=[pltpu.VMEM((2 * width, tok_rows), jnp.bfloat16)],
        compiler_params=alone,
        name="dispatch",
    )(expert_ids.T, gate_values.T, tokens.T, cotangent.T)
    send, gate_w, up_w, down_w = lax.optimization_barrier(
        (send, gate_weight[0], up_weight[0], down_weight[0].T)
    )
    half = jax.ShapeDtypeStruct((width + width // 2, hidden), jnp.bfloat16)
    low, high = pl.pallas_call(
        pack_kernel,
        out_shape=(half, half),
        compiler_params=params,
        name="pack",
    )(gate_w, up_w, down_w)
    low_1 = lax.ppermute(low, AXES, onward)
    high_3 = lax.ppermute(high, AXES, back)
    high_1 = lax.ppermute(high, AXES, onward)
    low_3 = lax.ppermute(low, AXES, back)
    low_2 = lax.ppermute(low_1, AXES, onward)
    high_2 = lax.ppermute(high_3, AXES, back)
    weights = (low, high, low_1, high_1, low_3, high_3, low_2, high_2)
    recv = lax.all_to_all(
        send.reshape(held, CAP, 2 * width), "expert", split_axis=0, concat_axis=0, tiled=True
    ).reshape(slots, 2 * width)

    mine = exchange(recv.reshape(SIDE, wide, 2 * width), first)
    vmem = pl.BlockSpec(memory_space=pltpu.VMEM)
    smem = pl.BlockSpec(memory_space=pltpu.SMEM)
    anywhere = pl.BlockSpec(memory_space=pl.ANY)
    others = 2 * (SIDE - 1)
    sums = pl.pallas_call(
        partial_kernel,
        in_specs=[smem] + [vmem] * 3 + [anywhere] * others,
        out_specs=vmem,
        out_shape=jax.ShapeDtypeStruct((wide, coded), jnp.int16),
        scratch_shapes=[pltpu.VMEM((width + width // 2, hidden), jnp.bfloat16)] * others
        + [pltpu.SemaphoreType.DMA((others,))],
        compiler_params=params,
        name="partials",
    )(place, mine, *weights)
    sums = exchange(sums.reshape(SIDE, rows, coded), second)
    grads = pl.pallas_call(
        lambda *refs: local_kernel(hidden, *refs),
        out_shape=jax.ShapeDtypeStruct((SIDE, rows, 2 * hidden), jnp.bfloat16),
        compiler_params=params,
        name="local_grads",
    )(sums)
    grads = exchange(grads, second).reshape(wide, 2 * hidden)
    row_grads = pl.pallas_call(
        row_kernel,
        in_specs=[smem] + [vmem] * 3 + [anywhere] * others,
        out_specs=vmem,
        out_shape=jax.ShapeDtypeStruct((SIDE, wide // 2, 2 * width), jnp.bfloat16),
        scratch_shapes=[pltpu.VMEM((width, hidden), jnp.bfloat16)] * others
        + [pltpu.SemaphoreType.DMA((others,))],
        compiler_params=params,
        name="row_grads",
    )(place, grads, *weights)
    row_grads = exchange(row_grads, first)
    returned = lax.all_to_all(
        row_grads.reshape(held, CAP // 2, 2 * width),
        "expert",
        split_axis=0,
        concat_axis=0,
        tiled=True,
    ).reshape(slots // 2, 2 * width)

    blocks = [grads] + [lax.ppermute(grads, AXES, plane_ring(held, k)) for k in (1, 3, 2)]
    column = 2 * TILE
    per = hidden // column

    def weight_grad(first_column):
        return pl.pallas_call(
            weight_kernel,
            grid=(per,),
            in_specs=[
                pl.BlockSpec(memory_space=pltpu.SMEM),
                pl.BlockSpec((SIDE, wide, 2 * width), lambda i: (0, 0, 0)),
            ]
            + [pl.BlockSpec((wide, column), lambda i: (0, i + first_column))] * SIDE,
            out_specs=pl.BlockSpec((1, width, column), lambda i: (0, 0, i)),
            out_shape=jax.ShapeDtypeStruct((1, width, hidden), jnp.bfloat16),
            compiler_params=params,
            name="weight_grad",
        )(place, recv.reshape(SIDE, wide, 2 * width), *blocks)

    gate_grad, up_grad = weight_grad(0), weight_grad(per)
    returned, gate_grad, up_grad = lax.optimization_barrier((returned, gate_grad, up_grad))
    token_grad = pl.pallas_call(
        combine_kernel,
        out_shape=jax.ShapeDtypeStruct((width, tok_rows), jnp.bfloat16),
        compiler_params=params,
        name="combine",
    )(returned, member).T
    return (token_grad, gate_grad, up_grad)


def solution(mesh):
    placed = (
        P("expert", "dp"),
        P("expert", "dp"),
        P("expert", "dp", None),
        P("expert", "dp", None),
        P("expert", None, "dp"),
        P("expert", None),
        P("expert", None),
    )
    return jax.shard_map(
        body,
        mesh=mesh,
        in_specs=placed,
        out_specs=(P("expert", "dp"), P("expert", "dp", None), P("expert", "dp", None)),
        check_vma=False,
    )
```

```python
import jax
import jax.numpy as jnp
from jax import lax
from jax.experimental import pallas as pl
from jax.experimental.pallas import tpu as pltpu
from jax.sharding import PartitionSpec as P

CAP = 16
SIDE = 4
TILE = 256
MIB = 1 << 20
AXES = ("expert", "dp")
ACROSS = (((1,), (1,)), ((), ()))
DOWN = (((0,), (0,)), ((), ()))
SHIFTS = (0, 3, 1, 2)


def block_at(ref, at):
    block = ref[0]
    for p in range(1, SIDE):
        block = jnp.where(at == p, ref[p], block)
    return block


def dispatch_kernel(ids_ref, gates_ref, tokens_ref, cotangent_ref, send_ref, member_ref, both):
    top_count, tok_rows = ids_ref.shape
    width = tokens_ref.shape[0]
    slots = send_ref.shape[0]
    held = slots // CAP
    ids = ids_ref[...]
    gates = gates_ref[...]
    expert = lax.broadcasted_iota(jnp.int32, (held, tok_rows), 0)
    named = jnp.zeros((held, tok_rows), jnp.float32)
    gate = jnp.zeros((held, tok_rows), jnp.float32)
    for k in range(top_count):
        hit = ids[k : k + 1, :] == expert
        named = jnp.where(hit, 1.0, named)
        gate = jnp.where(hit, gates[k : k + 1, :], gate)
    earlier = lax.broadcasted_iota(jnp.int32, (tok_rows, tok_rows), 0) < lax.broadcasted_iota(
        jnp.int32, (tok_rows, tok_rows), 1
    )
    rank = jnp.dot(
        named.astype(jnp.bfloat16),
        jnp.where(earlier, 1.0, 0.0).astype(jnp.bfloat16),
        preferred_element_type=jnp.float32,
    )
    code = jnp.where(named > 0.0, rank, -1.0)

    def by_slot(table):
        return jnp.broadcast_to(table[:, None, :], (held, CAP, tok_rows)).reshape(slots, tok_rows)

    slot = (lax.broadcasted_iota(jnp.int32, (slots, tok_rows), 0) % CAP).astype(jnp.float32)
    placed = by_slot(code) == slot
    slot_gate = jnp.sum(jnp.where(placed, by_slot(gate), 0.0), axis=1, keepdims=True)
    member = jnp.where(placed, 1.0, 0.0)
    halves = member.reshape(held, 2, CAP // 2, tok_rows)
    for i in (0, 1):
        member_ref[i] = halves[:, i].reshape(slots // 2, tok_rows).astype(jnp.bfloat16)
    member = member.astype(jnp.bfloat16)
    both[:width, :] = tokens_ref[...]
    both[width:, :] = cotangent_ref[...]
    picked = lax.dot_general(member, both[...], ACROSS, preferred_element_type=jnp.float32)
    column = lax.broadcasted_iota(jnp.int32, picked.shape, 1)
    send_ref[...] = jnp.where(column < width, picked, picked * slot_gate).astype(jnp.bfloat16)


def put_coded(out_ref, values):
    rows, cols = values[0].shape
    lane = lax.broadcasted_iota(jnp.int32, (rows, 128), 1)
    powers = jnp.zeros((rows, 128), jnp.float32)
    for i, value in enumerate(values):
        most = jnp.max(jnp.abs(value), axis=1, keepdims=True)
        power = jnp.floor(jnp.log2(jnp.maximum(most, 1e-30)))
        coded = jnp.round(value * jnp.exp2(13.0 - power)).astype(jnp.int32).astype(jnp.int16)
        out_ref[:, i * cols : (i + 1) * cols] = coded
        powers = jnp.where(lane == i, power, powers)
    out_ref[:, len(values) * cols :] = powers.astype(jnp.int32).astype(jnp.int16)


def sum_coded(parts_ref, cols):
    count = parts_ref.shape[2] // cols
    totals = [None] * count
    for p in range(parts_ref.shape[0]):
        powers = parts_ref[p, :, count * cols :].astype(jnp.int32).astype(jnp.float32)
        for i in range(count):
            unit = jnp.exp2(powers[:, i : i + 1] - 13.0)
            coded = parts_ref[p, :, i * cols : (i + 1) * cols].astype(jnp.int32)
            value = coded.astype(jnp.float32) * unit
            totals[i] = value if p == 0 else totals[i] + value
    return totals


def fetch(arrays, buffers, sems):
    copies = []
    for i, (array, buffer) in enumerate(zip(arrays, buffers)):
        source = array.at[: buffer.shape[0]]
        copies.append(pltpu.make_async_copy(source, buffer, sems.at[i]))
        copies[-1].start()

    def ready(i):
        copies[i].wait()
        return buffers[i]

    return ready


def pack_kernel(up_ref, down_ref, ups_ref):
    width = up_ref.shape[0]
    ups_ref[:width] = up_ref[...]
    ups_ref[width:] = down_ref[...]


def far_kernel(place_ref, recv_ref, ups_ref, out_ref):
    width = recv_ref.shape[2] // 2
    g = block_at(recv_ref, lax.rem(place_ref[0] + 2, SIDE))[:, width:]
    put_coded(out_ref, [jnp.dot(g, ups_ref[width:], preferred_element_type=jnp.float32)])


def partial_kernel(place_ref, rows_ref, far_ref, own_ups, *refs):
    count = (len(refs) - 2) // 2
    out_ref = refs[count]
    ready = fetch(refs[:count], refs[count + 1 : -1], refs[-1])
    width = rows_ref.shape[2] // 2
    totals = [None, None, sum_coded(far_ref, own_ups.shape[1])[0]]

    def add(which, rows, weight):
        value = jnp.dot(rows, weight, preferred_element_type=jnp.float32)
        totals[which] = value if totals[which] is None else totals[which] + value

    def rows_of(i):
        both = block_at(rows_ref, lax.rem(place_ref[0] + SHIFTS[i], SIDE))
        return both[:, :width], both[:, width:]

    x, g = rows_of(0)
    add(1, x, own_ups[:width])
    add(2, g, own_ups[width:])
    add(0, x, ready(0)[...])
    x, g = rows_of(1)
    add(0, x, ready(1)[...])
    ups = ready(2)
    add(1, x, ups[:width])
    add(2, g, ups[width:])
    x, g = rows_of(2)
    add(1, x, ready(3)[...])
    add(0, x, ready(4)[...])
    add(2, g, ready(5)[...])
    x, _ = rows_of(3)
    add(0, x, ready(6)[...])
    add(1, x, ready(7)[...])
    put_coded(out_ref, totals)


def local_kernel(hidden, parts_ref, out_ref):
    gate_act, up_act, back_act = sum_coded(parts_ref, hidden)
    sig = 1.0 / (1.0 + jnp.exp(-gate_act))
    grad_gate = (back_act * up_act * sig * (1.0 + gate_act * (1.0 - sig))).astype(jnp.bfloat16)
    grad_up = (back_act * gate_act * sig).astype(jnp.bfloat16)
    for p in range(out_ref.shape[0]):
        out_ref[p, :, :hidden] = grad_gate
        out_ref[p, :, hidden:] = grad_up


def row_kernel(place_ref, grads_ref, own_ups, *refs):
    count = (len(refs) - 2) // 2
    out_ref = refs[count]
    ready = fetch(refs[:count], refs[count + 1 : -1], refs[-1])
    wide, hidden = grads_ref.shape[0], grads_ref.shape[1] // 2
    width = out_ref.shape[2] // 2
    order = ((0, None), (1, 2), (4, 3), (5, 6))
    values = []
    for pair in order:
        total = None
        for j in (1, 0):
            value = lax.dot_general(
                grads_ref[:, j * hidden : (j + 1) * hidden],
                (own_ups if pair[j] is None else ready(pair[j]))[:width],
                ACROSS,
                preferred_element_type=jnp.float32,
            )
            total = value if total is None else total + value
        both = total.reshape(-1, 2, CAP // 2, width)
        pair = [both[:, j].reshape(wide // 2, width) for j in (0, 1)]
        values.append(jnp.concatenate(pair, axis=1).astype(jnp.bfloat16))
    for p in range(SIDE):
        block = values[0]
        for shift, value in zip(SHIFTS[1:], values[1:]):
            block = jnp.where(lax.rem(place_ref[0] + shift, SIDE) == p, value, block)
        out_ref[p] = block


def weight_kernel(place_ref, rows_ref, *refs):
    grads, out_ref = refs[:SIDE], refs[SIDE]
    width = out_ref.shape[1]
    value = None
    for shift, grad in zip(SHIFTS, grads):
        rows = block_at(rows_ref, lax.rem(place_ref[0] + shift, SIDE))[:, :width]
        term = lax.dot_general(rows, grad[...], DOWN, preferred_element_type=jnp.float32)
        value = term if value is None else value + term
    out_ref[0] = value.astype(jnp.bfloat16)


def combine_kernel(returned_ref, member_ref, out_ref):
    width = out_ref.shape[0]
    out_ref[...] = (
        lax.dot_general(
            returned_ref[:, :width], member_ref[0], DOWN, preferred_element_type=jnp.float32
        )
        + lax.dot_general(
            returned_ref[:, width:], member_ref[1], DOWN, preferred_element_type=jnp.float32
        )
    ).astype(jnp.bfloat16)


def plane_groups(held, swap):
    groups = []
    for e in range(held):
        for other in range(SIDE):
            if (e % 2 == 1) == swap:
                group = [(e * SIDE + a) * SIDE + other for a in range(SIDE)]
            else:
                group = [(e * SIDE + other) * SIDE + a for a in range(SIDE)]
            groups.append(group)
    return groups


def plane_ring(held, step):
    pairs = []
    for group in plane_groups(held, False):
        pairs += [(group[i], group[(i + step) % SIDE]) for i in range(SIDE)]
    return pairs


def exchange(blocks, groups):
    return lax.all_to_all(
        blocks, AXES, split_axis=0, concat_axis=0, tiled=True, axis_index_groups=groups
    )


def body(tokens, cotangent, gate_weight, up_weight, down_weight, expert_ids, gate_values):
    held = lax.axis_size("expert")
    tok_rows, width = tokens.shape
    slots = held * CAP
    hidden = gate_weight.shape[2]
    first, second = plane_groups(held, False), plane_groups(held, True)
    wide = slots // SIDE
    rows = wide // SIDE
    coded = 3 * hidden + 128
    params = pltpu.CompilerParams(vmem_limit_bytes=24 * MIB)
    alone = pltpu.CompilerParams(vmem_limit_bytes=56 * MIB)

    onward, back = plane_ring(held, 1), plane_ring(held, -1)
    dp = lax.axis_index("dp")
    place = jnp.where(lax.axis_index("expert") % 2 == 0, dp // SIDE, dp % SIDE)
    place = place.astype(jnp.int32).reshape(1)

    send, member = pl.pallas_call(
        dispatch_kernel,
        out_shape=(
            jax.ShapeDtypeStruct((slots, 2 * width), jnp.bfloat16),
            jax.ShapeDtypeStruct((2, slots // 2, tok_rows), jnp.bfloat16),
        ),
        scratch_shapes=[pltpu.VMEM((2 * width, tok_rows), jnp.bfloat16)],
        compiler_params=alone,
        name="dispatch",
    )(expert_ids.T, gate_values.T, tokens.T, cotangent.T)
    send, gate, up, down = lax.optimization_barrier(
        (send, gate_weight[0], up_weight[0], down_weight[0].T)
    )

    def on(array):
        return lax.ppermute(array, AXES, onward)

    def off(array):
        return lax.ppermute(array, AXES, back)

    gate_1, up_3 = on(gate), off(up)
    ups = pl.pallas_call(
        pack_kernel,
        out_shape=jax.ShapeDtypeStruct((2 * width, hidden), jnp.bfloat16),
        compiler_params=params,
        name="pack",
    )(up, down)
    ups_1, gate_3, down_3 = on(ups), off(gate), off(down)
    gate_2, up_2 = on(gate_1), off(up_3)
    forward = (gate, gate_1, ups_1, up_3, gate_3, down_3, gate_2, up_2)
    backward = (gate, gate_1, ups_1, up_3, gate_3, gate_2, up_2)

    recv = lax.all_to_all(
        send.reshape(held, CAP, 2 * width), "expert", split_axis=0, concat_axis=0, tiled=True
    ).reshape(slots, 2 * width)

    vmem = pl.BlockSpec(memory_space=pltpu.VMEM)
    smem = pl.BlockSpec(memory_space=pltpu.SMEM)
    anywhere = pl.BlockSpec(memory_space=pl.ANY)

    def buffers(shapes):
        return [pltpu.VMEM(shape, jnp.bfloat16) for shape in shapes] + [
            pltpu.SemaphoreType.DMA((len(shapes),))
        ]

    mine = exchange(recv.reshape(SIDE, wide, 2 * width), first)
    far = pl.pallas_call(
        far_kernel,
        in_specs=[smem, vmem, vmem],
        out_specs=vmem,
        out_shape=jax.ShapeDtypeStruct((wide, hidden + 128), jnp.int16),
        compiler_params=params,
        name="far_products",
    )(place, recv.reshape(SIDE, wide, 2 * width), ups)
    far = lax.ppermute(far, AXES, plane_ring(held, 2))
    sums = pl.pallas_call(
        partial_kernel,
        in_specs=[smem] + [vmem] * 3 + [anywhere] * len(forward),
        out_specs=vmem,
        out_shape=jax.ShapeDtypeStruct((wide, coded), jnp.int16),
        scratch_shapes=buffers([x.shape for x in forward]),
        compiler_params=params,
        name="partials",
    )(place, mine, far[None], ups, *forward)
    sums = exchange(sums.reshape(SIDE, rows, coded), second)
    grads = pl.pallas_call(
        lambda *refs: local_kernel(hidden, *refs),
        out_shape=jax.ShapeDtypeStruct((SIDE, rows, 2 * hidden), jnp.bfloat16),
        compiler_params=params,
        name="local_grads",
    )(sums)
    grads = exchange(grads, second).reshape(wide, 2 * hidden)
    row_grads = pl.pallas_call(
        row_kernel,
        in_specs=[smem] + [vmem] * 2 + [anywhere] * len(backward),
        out_specs=vmem,
        out_shape=jax.ShapeDtypeStruct((SIDE, wide // 2, 2 * width), jnp.bfloat16),
        scratch_shapes=buffers([(width, hidden)] * len(backward)),
        compiler_params=params,
        name="row_grads",
    )(place, grads, ups, *backward)
    row_grads = exchange(row_grads, first)
    returned = lax.all_to_all(
        row_grads.reshape(held, CAP // 2, 2 * width),
        "expert",
        split_axis=0,
        concat_axis=0,
        tiled=True,
    ).reshape(slots // 2, 2 * width)

    blocks = [grads] + [lax.ppermute(grads, AXES, plane_ring(held, k)) for k in (1, 3, 2)]
    column = 2 * TILE
    per = hidden // column

    def weight_grad(first_column):
        return pl.pallas_call(
            weight_kernel,
            grid=(per,),
            in_specs=[
                pl.BlockSpec(memory_space=pltpu.SMEM),
                pl.BlockSpec((SIDE, wide, 2 * width), lambda i: (0, 0, 0)),
            ]
            + [pl.BlockSpec((wide, column), lambda i: (0, i + first_column))] * SIDE,
            out_specs=pl.BlockSpec((1, width, column), lambda i: (0, 0, i)),
            out_shape=jax.ShapeDtypeStruct((1, width, hidden), jnp.bfloat16),
            compiler_params=params,
            name="weight_grad",
        )(place, recv.reshape(SIDE, wide, 2 * width), *blocks)

    gate_grad, up_grad = weight_grad(0), weight_grad(per)
    returned, gate_grad, up_grad = lax.optimization_barrier((returned, gate_grad, up_grad))
    token_grad = pl.pallas_call(
        combine_kernel,
        out_shape=jax.ShapeDtypeStruct((width, tok_rows), jnp.bfloat16),
        compiler_params=params,
        name="combine",
    )(returned, member).T
    return (token_grad, gate_grad, up_grad)


def solution(mesh):
    placed = (
        P("expert", "dp"),
        P("expert", "dp"),
        P("expert", "dp", None),
        P("expert", "dp", None),
        P("expert", None, "dp"),
        P("expert", None),
        P("expert", None),
    )
    return jax.shard_map(
        body,
        mesh=mesh,
        in_specs=placed,
        out_specs=(P("expert", "dp"), P("expert", "dp", None), P("expert", "dp", None)),
        check_vma=False,
    )
```

```python
import jax
import jax.numpy as jnp
from jax import lax
from jax.experimental import pallas as pl
from jax.experimental.pallas import tpu as pltpu
from jax.sharding import PartitionSpec as P

CAP = 16
SIDE = 4
TILE = 256
MIB = 1 << 20
AXES = ("expert", "dp")
ACROSS = (((1,), (1,)), ((), ()))
DOWN = (((0,), (0,)), ((), ()))
SHIFTS = (0, 3, 1, 2)


def block_at(ref, at):
    block = ref[0]
    for p in range(1, SIDE):
        block = jnp.where(at == p, ref[p], block)
    return block


def dispatch_kernel(
    ids_hbm,
    gates_hbm,
    tokens_hbm,
    cotangent_hbm,
    send_hbm,
    member_hbm,
    ids_ref,
    gates_ref,
    both,
    send_ref,
    member_ref,
    sems,
):
    top_count, tok_rows = ids_ref.shape
    width = tokens_hbm.shape[0]
    slots = send_ref.shape[0]
    loads = [
        pltpu.make_async_copy(source, target, sems.at[i])
        for i, (source, target) in enumerate(
            (
                (ids_hbm, ids_ref),
                (gates_hbm, gates_ref),
                (tokens_hbm, both.at[:width]),
                (cotangent_hbm, both.at[width:]),
            )
        )
    ]
    for load in loads:
        load.start()
    loads[0].wait()
    loads[1].wait()
    held = slots // CAP
    ids = ids_ref[...]
    gates = gates_ref[...]
    expert = lax.broadcasted_iota(jnp.int32, (held, tok_rows), 0)
    named = jnp.zeros((held, tok_rows), jnp.float32)
    gate = jnp.zeros((held, tok_rows), jnp.float32)
    for k in range(top_count):
        hit = ids[k : k + 1, :] == expert
        named = jnp.where(hit, 1.0, named)
        gate = jnp.where(hit, gates[k : k + 1, :], gate)
    earlier = lax.broadcasted_iota(jnp.int32, (tok_rows, tok_rows), 0) < lax.broadcasted_iota(
        jnp.int32, (tok_rows, tok_rows), 1
    )
    rank = jnp.dot(
        named.astype(jnp.bfloat16),
        jnp.where(earlier, 1.0, 0.0).astype(jnp.bfloat16),
        preferred_element_type=jnp.float32,
    )
    code = jnp.where(named > 0.0, rank, -1.0)

    def by_slot(table):
        return jnp.broadcast_to(table[:, None, :], (held, CAP, tok_rows)).reshape(slots, tok_rows)

    slot = (lax.broadcasted_iota(jnp.int32, (slots, tok_rows), 0) % CAP).astype(jnp.float32)
    placed = by_slot(code) == slot
    slot_gate = jnp.sum(jnp.where(placed, by_slot(gate), 0.0), axis=1, keepdims=True)
    member = jnp.where(placed, 1.0, 0.0)
    halves = member.reshape(held, 2, CAP // 2, tok_rows)
    for i in (0, 1):
        member_ref[i] = halves[:, i].reshape(slots // 2, tok_rows).astype(jnp.bfloat16)
    member = member.astype(jnp.bfloat16)
    stores = [pltpu.make_async_copy(member_ref, member_hbm, sems.at[4])]
    stores[0].start()
    loads[2].wait()
    loads[3].wait()
    column = lax.broadcasted_iota(jnp.int32, (slots // 2, 2 * width), 1)
    for i in (0, 1):
        part = slice(i * slots // 2, (i + 1) * slots // 2)
        picked = lax.dot_general(
            member[part], both[...], ACROSS, preferred_element_type=jnp.float32
        )
        scaled = picked * slot_gate[part]
        send_ref[part] = jnp.where(column < width, picked, scaled).astype(jnp.bfloat16)
        stores.append(
            pltpu.make_async_copy(send_ref.at[part], send_hbm.at[part], sems.at[5 + i])
        )
        stores[-1].start()
    for store in stores:
        store.wait()


def put_coded(out_ref, values):
    rows, cols = values[0].shape
    lane = lax.broadcasted_iota(jnp.int32, (rows, 128), 1)
    powers = jnp.zeros((rows, 128), jnp.float32)
    for i, value in enumerate(values):
        most = jnp.max(jnp.abs(value), axis=1, keepdims=True)
        power = jnp.floor(jnp.log2(jnp.maximum(most, 1e-30)))
        coded = jnp.round(value * jnp.exp2(13.0 - power)).astype(jnp.int32).astype(jnp.int16)
        out_ref[:, i * cols : (i + 1) * cols] = coded
        powers = jnp.where(lane == i, power, powers)
    out_ref[:, len(values) * cols :] = powers.astype(jnp.int32).astype(jnp.int16)


def sum_coded(parts_ref, cols):
    count = parts_ref.shape[2] // cols
    totals = [None] * count
    for p in range(parts_ref.shape[0]):
        powers = parts_ref[p, :, count * cols :].astype(jnp.int32).astype(jnp.float32)
        for i in range(count):
            unit = jnp.exp2(powers[:, i : i + 1] - 13.0)
            coded = parts_ref[p, :, i * cols : (i + 1) * cols].astype(jnp.int32)
            value = coded.astype(jnp.float32) * unit
            totals[i] = value if p == 0 else totals[i] + value
    return totals


def fetch(arrays, buffers, sems):
    copies = []
    for i, (array, buffer) in enumerate(zip(arrays, buffers)):
        source = array.at[: buffer.shape[0]]
        copies.append(pltpu.make_async_copy(source, buffer, sems.at[i]))
        copies[-1].start()

    def ready(i):
        copies[i].wait()
        return buffers[i]

    return ready


def pack_kernel(up_ref, down_ref, ups_ref):
    width = up_ref.shape[0]
    ups_ref[:width] = up_ref[...]
    ups_ref[width:] = down_ref[...]


def far_kernel(place_ref, recv_ref, ups_ref, out_ref):
    width = recv_ref.shape[2] // 2
    g = block_at(recv_ref, lax.rem(place_ref[0] + 2, SIDE))[:, width:]
    put_coded(out_ref, [jnp.dot(g, ups_ref[width:], preferred_element_type=jnp.float32)])


def partial_kernel(place_ref, rows_ref, far_ref, own_ups, *refs):
    count = (len(refs) - 2) // 2
    out_ref = refs[count]
    ready = fetch(refs[:count], refs[count + 1 : -1], refs[-1])
    width = rows_ref.shape[2] // 2
    totals = [None, None, sum_coded(far_ref, own_ups.shape[1])[0]]

    def add(which, rows, weight):
        value = jnp.dot(rows, weight, preferred_element_type=jnp.float32)
        totals[which] = value if totals[which] is None else totals[which] + value

    def rows_of(i):
        both = block_at(rows_ref, lax.rem(place_ref[0] + SHIFTS[i], SIDE))
        return both[:, :width], both[:, width:]

    x, g = rows_of(0)
    add(1, x, own_ups[:width])
    add(2, g, own_ups[width:])
    add(0, x, ready(0)[...])
    x, g = rows_of(1)
    add(0, x, ready(1)[...])
    ups = ready(2)
    add(1, x, ups[:width])
    add(2, g, ups[width:])
    x, g = rows_of(2)
    add(1, x, ready(3)[...])
    add(0, x, ready(4)[...])
    add(2, g, ready(5)[...])
    x, _ = rows_of(3)
    add(0, x, ready(6)[...])
    add(1, x, ready(7)[...])
    put_coded(out_ref, totals)


def local_kernel(hidden, parts_ref, out_ref):
    gate_act, up_act, back_act = sum_coded(parts_ref, hidden)
    sig = 1.0 / (1.0 + jnp.exp(-gate_act))
    grad_gate = (back_act * up_act * sig * (1.0 + gate_act * (1.0 - sig))).astype(jnp.bfloat16)
    grad_up = (back_act * gate_act * sig).astype(jnp.bfloat16)
    for p in range(out_ref.shape[0]):
        out_ref[p, :, :hidden] = grad_gate
        out_ref[p, :, hidden:] = grad_up


def row_kernel(place_ref, grads_ref, own_ups, *refs):
    count = (len(refs) - 2) // 2
    out_ref = refs[count]
    ready = fetch(refs[:count], refs[count + 1 : -1], refs[-1])
    wide, hidden = grads_ref.shape[0], grads_ref.shape[1] // 2
    width = out_ref.shape[2] // 2
    order = ((0, None), (1, 2), (4, 3), (5, 6))
    values = []
    for pair in order:
        total = None
        for j in (1, 0):
            value = lax.dot_general(
                grads_ref[:, j * hidden : (j + 1) * hidden],
                (own_ups if pair[j] is None else ready(pair[j]))[:width],
                ACROSS,
                preferred_element_type=jnp.float32,
            )
            total = value if total is None else total + value
        both = total.reshape(-1, 2, CAP // 2, width)
        pair = [both[:, j].reshape(wide // 2, width) for j in (0, 1)]
        values.append(jnp.concatenate(pair, axis=1).astype(jnp.bfloat16))
    for p in range(SIDE):
        block = values[0]
        for shift, value in zip(SHIFTS[1:], values[1:]):
            block = jnp.where(lax.rem(place_ref[0] + shift, SIDE) == p, value, block)
        out_ref[p] = block


def weight_kernel(place_ref, rows_ref, *refs):
    grads, out_ref = refs[:SIDE], refs[SIDE]
    width = out_ref.shape[1]
    value = None
    for shift, grad in zip(SHIFTS, grads):
        rows = block_at(rows_ref, lax.rem(place_ref[0] + shift, SIDE))[:, :width]
        term = lax.dot_general(rows, grad[...], DOWN, preferred_element_type=jnp.float32)
        value = term if value is None else value + term
    out_ref[0] = value.astype(jnp.bfloat16)


def combine_kernel(returned_ref, member_ref, out_ref):
    width = out_ref.shape[0]
    out_ref[...] = (
        lax.dot_general(
            returned_ref[:, :width], member_ref[0], DOWN, preferred_element_type=jnp.float32
        )
        + lax.dot_general(
            returned_ref[:, width:], member_ref[1], DOWN, preferred_element_type=jnp.float32
        )
    ).astype(jnp.bfloat16)


def plane_groups(held, swap):
    groups = []
    for e in range(held):
        for other in range(SIDE):
            if (e % 2 == 1) == swap:
                group = [(e * SIDE + a) * SIDE + other for a in range(SIDE)]
            else:
                group = [(e * SIDE + other) * SIDE + a for a in range(SIDE)]
            groups.append(group)
    return groups


def plane_ring(held, step):
    pairs = []
    for group in plane_groups(held, False):
        pairs += [(group[i], group[(i + step) % SIDE]) for i in range(SIDE)]
    return pairs


def exchange(blocks, groups):
    return lax.all_to_all(
        blocks, AXES, split_axis=0, concat_axis=0, tiled=True, axis_index_groups=groups
    )


def body(tokens, cotangent, gate_weight, up_weight, down_weight, expert_ids, gate_values):
    held = lax.axis_size("expert")
    tok_rows, width = tokens.shape
    slots = held * CAP
    hidden = gate_weight.shape[2]
    first, second = plane_groups(held, False), plane_groups(held, True)
    wide = slots // SIDE
    rows = wide // SIDE
    coded = 3 * hidden + 128
    params = pltpu.CompilerParams(vmem_limit_bytes=24 * MIB)
    alone = pltpu.CompilerParams(vmem_limit_bytes=56 * MIB)

    onward, back = plane_ring(held, 1), plane_ring(held, -1)
    dp = lax.axis_index("dp")
    place = jnp.where(lax.axis_index("expert") % 2 == 0, dp // SIDE, dp % SIDE)
    place = place.astype(jnp.int32).reshape(1)

    send, member = pl.pallas_call(
        dispatch_kernel,
        out_shape=(
            jax.ShapeDtypeStruct((slots, 2 * width), jnp.bfloat16),
            jax.ShapeDtypeStruct((2, slots // 2, tok_rows), jnp.bfloat16),
        ),
        in_specs=[pl.BlockSpec(memory_space=pl.ANY)] * 4,
        out_specs=[pl.BlockSpec(memory_space=pl.ANY)] * 2,
        scratch_shapes=[
            pltpu.VMEM(expert_ids.shape[::-1], jnp.int32),
            pltpu.VMEM(gate_values.shape[::-1], jnp.float32),
            pltpu.VMEM((2 * width, tok_rows), jnp.bfloat16),
            pltpu.VMEM((slots, 2 * width), jnp.bfloat16),
            pltpu.VMEM((2, slots // 2, tok_rows), jnp.bfloat16),
            pltpu.SemaphoreType.DMA((7,)),
        ],
        compiler_params=alone,
        name="dispatch",
    )(expert_ids.T, gate_values.T, tokens.T, cotangent.T)
    send, gate, up, down = lax.optimization_barrier(
        (send, gate_weight[0], up_weight[0], down_weight[0].T)
    )

    def on(array):
        return lax.ppermute(array, AXES, onward)

    def off(array):
        return lax.ppermute(array, AXES, back)

    gate_1, up_3 = on(gate), off(up)
    ups = pl.pallas_call(
        pack_kernel,
        out_shape=jax.ShapeDtypeStruct((2 * width, hidden), jnp.bfloat16),
        compiler_params=params,
        name="pack",
    )(up, down)
    ups_1, gate_3, down_3 = on(ups), off(gate), off(down)
    gate_2, up_2 = on(gate_1), off(up_3)
    forward = (gate, gate_1, ups_1, up_3, gate_3, down_3, gate_2, up_2)
    backward = (gate, gate_1, ups_1, up_3, gate_3, gate_2, up_2)

    recv = lax.all_to_all(
        send.reshape(held, CAP, 2 * width), "expert", split_axis=0, concat_axis=0, tiled=True
    ).reshape(slots, 2 * width)

    vmem = pl.BlockSpec(memory_space=pltpu.VMEM)
    smem = pl.BlockSpec(memory_space=pltpu.SMEM)
    anywhere = pl.BlockSpec(memory_space=pl.ANY)

    def buffers(shapes):
        return [pltpu.VMEM(shape, jnp.bfloat16) for shape in shapes] + [
            pltpu.SemaphoreType.DMA((len(shapes),))
        ]

    mine = exchange(recv.reshape(SIDE, wide, 2 * width), first)
    far = pl.pallas_call(
        far_kernel,
        in_specs=[smem, vmem, vmem],
        out_specs=vmem,
        out_shape=jax.ShapeDtypeStruct((wide, hidden + 128), jnp.int16),
        compiler_params=params,
        name="far_products",
    )(place, recv.reshape(SIDE, wide, 2 * width), ups)
    far = lax.ppermute(far, AXES, plane_ring(held, 2))
    sums = pl.pallas_call(
        partial_kernel,
        in_specs=[smem] + [vmem] * 3 + [anywhere] * len(forward),
        out_specs=vmem,
        out_shape=jax.ShapeDtypeStruct((wide, coded), jnp.int16),
        scratch_shapes=buffers([x.shape for x in forward]),
        compiler_params=params,
        name="partials",
    )(place, mine, far[None], ups, *forward)
    sums = exchange(sums.reshape(SIDE, rows, coded), second)
    grads = pl.pallas_call(
        lambda *refs: local_kernel(hidden, *refs),
        out_shape=jax.ShapeDtypeStruct((SIDE, rows, 2 * hidden), jnp.bfloat16),
        compiler_params=params,
        name="local_grads",
    )(sums)
    grads = exchange(grads, second).reshape(wide, 2 * hidden)
    row_grads = pl.pallas_call(
        row_kernel,
        in_specs=[smem] + [vmem] * 2 + [anywhere] * len(backward),
        out_specs=vmem,
        out_shape=jax.ShapeDtypeStruct((SIDE, wide // 2, 2 * width), jnp.bfloat16),
        scratch_shapes=buffers([(width, hidden)] * len(backward)),
        compiler_params=params,
        name="row_grads",
    )(place, grads, ups, *backward)
    row_grads = exchange(row_grads, first)
    returned = lax.all_to_all(
        row_grads.reshape(held, CAP // 2, 2 * width),
        "expert",
        split_axis=0,
        concat_axis=0,
        tiled=True,
    ).reshape(slots // 2, 2 * width)

    blocks = [grads] + [lax.ppermute(grads, AXES, plane_ring(held, k)) for k in (1, 3, 2)]
    column = 2 * TILE
    per = hidden // column

    def weight_grad(first_column):
        return pl.pallas_call(
            weight_kernel,
            grid=(per,),
            in_specs=[
                pl.BlockSpec(memory_space=pltpu.SMEM),
                pl.BlockSpec((SIDE, wide, 2 * width), lambda i: (0, 0, 0)),
            ]
            + [pl.BlockSpec((wide, column), lambda i: (0, i + first_column))] * SIDE,
            out_specs=pl.BlockSpec((1, width, column), lambda i: (0, 0, i)),
            out_shape=jax.ShapeDtypeStruct((1, width, hidden), jnp.bfloat16),
            compiler_params=params,
            name="weight_grad",
        )(place, recv.reshape(SIDE, wide, 2 * width), *blocks)

    gate_grad, up_grad = weight_grad(0), weight_grad(per)
    returned, gate_grad, up_grad = lax.optimization_barrier((returned, gate_grad, up_grad))
    token_grad = pl.pallas_call(
        combine_kernel,
        out_shape=jax.ShapeDtypeStruct((width, tok_rows), jnp.bfloat16),
        compiler_params=params,
        name="combine",
    )(returned, member).T
    return (token_grad, gate_grad, up_grad)


def solution(mesh):
    placed = (
        P("expert", "dp"),
        P("expert", "dp"),
        P("expert", "dp", None),
        P("expert", "dp", None),
        P("expert", None, "dp"),
        P("expert", None),
        P("expert", None),
    )
    return jax.shard_map(
        body,
        mesh=mesh,
        in_specs=placed,
        out_specs=(P("expert", "dp"), P("expert", "dp", None), P("expert", "dp", None)),
        check_vma=False,
    )
```
